32 devices in a mesh: dp: 16 (over z, y, x), head: 2 (over core).
Axes of the slice: x: 2, y: 2, z: 4, core: 2. Of those that a mesh axis runs over, the one named last changes fastest.
Arguments:
- hidden_in: float32 [6144, 1536], P(('dp', 'head')), may hold values from -6 to 6
- row_lengths: int32 [16, 3], P('dp'), may hold values from 0 to 384, as said below
- norm_attn: bfloat16 [1536], P('dp'), may hold values from 0.099609375 to 1.8984375
- w_query: bfloat16 [1536, 1536], P('dp', 'head'), may hold values from -0.15625 to 0.15625
- b_query: bfloat16 [2, 768], P('head', 'dp'), may hold values from -3 to 3
- w_key: bfloat16 [1536, 256], P('dp', 'head'), may hold values from -0.15625 to 0.15625
- b_key: bfloat16 [2, 128], P('head', 'dp'), may hold values from -3 to 3
- w_value: bfloat16 [1536, 256], P('dp', 'head'), may hold values from -0.15625 to 0.15625
- b_value: bfloat16 [2, 128], P('head', 'dp'), may hold values from -0.59765625 to 0.59765625
- w_out: bfloat16 [1536, 1536], P('head', 'dp'), may hold values from -1.25 to 1.25
- norm_mlp: bfloat16 [1536], P('dp'), may hold values from 0.099609375 to 1.8984375
- w_gate: bfloat16 [1536, 8960], P('dp', 'head'), may hold values from -0.15625 to 0.15625
- w_up: bfloat16 [1536, 8960], P('dp', 'head'), may hold values from -0.15625 to 0.15625
- w_down: bfloat16 [8960, 1536], P('head', 'dp'), may hold values from -0.125 to 0.125
- out_grad: float32 [6144, 1536], P(('dp', 'head')), may hold values from -18 to 18
Outputs:
- block_out: float32 [6144, 1536], P(('dp', 'head'))
- grad_in: float32 [6144, 1536], P(('dp', 'head'))
- grad_norm_attn: float32 [1536], replicated
- grad_w_query: float32 [1536, 1536], P('dp', 'head')
- grad_b_query: float32 [2, 768], replicated
- grad_w_key: float32 [1536, 256], P('dp', 'head')
- grad_b_key: float32 [2, 128], replicated
- grad_w_value: float32 [1536, 256], P('dp', 'head')
- grad_b_value: float32 [2, 128], replicated
- grad_w_out: float32 [1536, 1536], P('head', 'dp')
- grad_norm_mlp: float32 [1536], replicated
- grad_w_gate: float32 [1536, 8960], P('dp', 'head')
- grad_w_up: float32 [1536, 8960], P('dp', 'head')
- grad_w_down: float32 [8960, 1536], P('head', 'dp')
The draws below stay inside these ranges and needn't reach their ends.
Inputs may be any that keep to these rules, and one draw needn't show every extreme that they name: `row_lengths`: in every batch the nonzero lengths come first, are multiples of 96 and add up to 384, and the other slots are 0; some row of every batch holds both tokens 384 // 2 - 1 and 192 of the batch.
All inputs are finite; a program needn't handle non-finite values.
Results may differ from the reference program's by a relative error of at most 0.023.
Values may be sent and summed in bfloat16 or wider, within the bound.
A program may use at most 512 MiB of HBM per device.

```python
import math
import jax
import jax.numpy as jnp
from jax import lax

D = 1536
H = 12
KV = 2
HD = 128
FF = 8960
BATCH = 384
BATCHES = 16
TOKENS = 6144


def draw_row_lengths(key, part):
    quarter = BATCH // 4
    patterns = jnp.array([[4, 0, 0], [3, 1, 0], [1, 3, 0], [1, 2, 1]], dtype=jnp.int32) * quarter
    picked = jax.random.randint(key, (BATCHES,), 0, 4)
    forced = jax.random.randint(jax.random.fold_in(key, 7), (), 0, BATCHES)
    picked = jnp.where(jnp.arange(BATCHES) == forced, 0, picked)
    return patterns[picked]


def draw_out_grad(key, part):
    base_draw = jnp.clip(jax.random.normal(key, (TOKENS, D), jnp.float32), -6.0, 6.0)
    batch_of = (jnp.arange(TOKENS) // BATCH).astype(jnp.float32)
    lifted = 1.0 + 2.0 * batch_of / max(BATCHES - 1, 1)
    return base_draw * lifted[:, None]


def block_levels(own_key, dims, pieces, smallest, top_value):
    gain = 1.0
    for axis_at, parts in pieces:
        draws = jax.random.uniform(jax.random.fold_in(jax.random.fold_in(own_key, 6), axis_at), (parts,), jnp.float32, smallest / len(pieces), top_value / len(pieces))
        gain = gain * jnp.repeat(jnp.exp(draws), dims[axis_at] // parts).reshape((-1,) + (1,) * (len(dims) - 1 - axis_at))
    return gain


def centred(key, shape, width, limit, split=(), kind=jnp.bfloat16):
    result = width * jax.random.normal(key, shape, jnp.float32)
    if split:
        result = result * block_levels(key, shape, split, -0.22, 0.18)
    return jnp.clip(result, -limit, limit).astype(kind)


def setup_inputs(seed: int = 0) -> dict:
    key_list = jax.random.split(jax.random.key(seed), 16)
    hidden_in = centred(key_list[0], (TOKENS, D), 1.0, 6.0, ((0, 32),), jnp.float32)
    row_lengths = draw_row_lengths(jax.random.fold_in(key_list[15], 71), 0)
    norm_attn = jnp.clip(1.0 + 0.18 * jax.random.normal(key_list[2], (D,), jnp.float32), 0.099609375, 1.8984375).astype(jnp.bfloat16)
    w_query = centred(key_list[3], (D, H * HD), D ** -0.5, 0.15625, ((0, 16), (1, 2)))
    b_query = centred(key_list[4], (KV, H // KV * HD), 0.5, 3.0, ((0, 2), (1, 16)))
    w_key = centred(key_list[5], (D, KV * HD), D ** -0.5, 0.15625, ((0, 16), (1, 2)))
    b_key = centred(key_list[6], (KV, HD), 0.5, 3.0, ((0, 2), (1, 16)))
    w_value = centred(key_list[7], (D, KV * HD), D ** -0.5, 0.15625, ((0, 16), (1, 2)))
    b_value = centred(key_list[8], (KV, HD), 0.1, 0.59765625, ((0, 2), (1, 16)))
    w_out = centred(key_list[9], (H * HD, D), (H * HD // 64) ** -0.5, 1.25, ((0, 2), (1, 16)))
    norm_mlp = jnp.clip(1.0 + 0.18 * jax.random.normal(key_list[10], (D,), jnp.float32), 0.099609375, 1.8984375).astype(jnp.bfloat16)
    w_gate = centred(key_list[11], (D, FF), D ** -0.5, 0.15625, ((0, 16), (1, 2)))
    w_up = centred(key_list[12], (D, FF), D ** -0.5, 0.15625, ((0, 16), (1, 2)))
    w_down = centred(key_list[13], (FF, D), (FF // 4) ** -0.5, 0.125, ((0, 2), (1, 16)))
    out_grad = draw_out_grad(jax.random.fold_in(key_list[15], 71), 0)
    return dict(hidden_in=hidden_in, row_lengths=row_lengths, norm_attn=norm_attn, w_query=w_query, b_query=b_query, w_key=w_key, b_key=b_key, w_value=w_value, b_value=b_value, w_out=w_out, norm_mlp=norm_mlp, w_gate=w_gate, w_up=w_up, w_down=w_down, out_grad=out_grad)


NORM_EPS = 1e-06
ROPE_BASE = 1000000.0
MASKED = -1e+30

@jax.custom_vjp
def reduced_precision_cast(v):
    return lax.optimization_barrier(v.astype(jnp.bfloat16)).astype(jnp.float32)

@jax.custom_vjp
def reduced_precision_gradient(v):
    return v

def low_keep(v):
    return (reduced_precision_cast(v), None)

def low_pass(kept, grad):
    return (grad,)

def back_keep(v):
    return (v, None)

def back_low(kept, grad):
    return (reduced_precision_cast(grad),)
reduced_precision_cast.defvjp(low_keep, low_pass)
reduced_precision_gradient.defvjp(back_keep, back_low)

def matmul(left_side, right_side):
    return jnp.dot(left_side, right_side, precision=lax.Precision.HIGHEST)

def rms_norm(value_rows, gain_vec):
    return value_rows * lax.rsqrt(lax.optimization_barrier(jnp.mean(value_rows * value_rows, axis=-1, keepdims=True)) + NORM_EPS) * gain_vec

def layout(lengths_row, token_count):
    row_ends = jnp.cumsum(lengths_row).astype(jnp.int32)
    places = jnp.arange(token_count, dtype=jnp.int32)
    passed = (places[:, None] >= row_ends[None, :]).astype(jnp.int32)
    segment = lax.optimization_barrier(jnp.sum(passed, axis=1)).astype(jnp.int32)
    offset = lax.optimization_barrier(jnp.sum(passed * lengths_row[None, :], axis=1)).astype(jnp.int32)
    return (segment, places - offset, places)

def rotary_tables(positions, head_dim):
    half_dim = head_dim // 2
    frequency = jnp.exp(jnp.arange(half_dim, dtype=jnp.float32) * (-2.0 * math.log(ROPE_BASE) / head_dim))
    angles = positions.astype(jnp.float32)[:, None] * frequency[None, :]
    cosine = jnp.cos(angles)
    sine_tab = jnp.sin(angles)
    return (jnp.concatenate([cosine, cosine], -1), jnp.concatenate([sine_tab, sine_tab], -1))

def rotate(value_rows, cosine, sine_tab):
    half_dim = value_rows.shape[-1] // 2
    turned = jnp.concatenate([-value_rows[..., half_dim:], value_rows[..., :half_dim]], -1)
    return value_rows * cosine + turned * sine_tab

def block_layer(params, block_in, lengths_row):
    gain_attn, wq_full, bq_full, wk_full, bk_full, wv_full, bv_full, wo_full, gain_mlp, wg_full, wu_full, wd_full = params
    token_count = block_in.shape[0]
    segment, positions, places = layout(lengths_row, token_count)
    cosine, sine_tab = rotary_tables(positions, HD)
    cosine = cosine[:, None, :]
    sine_tab = sine_tab[:, None, :]
    normed = reduced_precision_cast(rms_norm(block_in, gain_attn))
    query_pre = reduced_precision_gradient(matmul(normed, wq_full) + bq_full.reshape(-1))
    key_pre = reduced_precision_gradient(matmul(normed, wk_full) + bk_full.reshape(-1))
    value_rows = reduced_precision_cast(reduced_precision_gradient(matmul(normed, wv_full) + bv_full.reshape(-1)))
    query_rows = reduced_precision_cast(rotate(query_pre.reshape(token_count, H, HD), cosine, sine_tab))
    query_rows = query_rows.reshape(token_count, KV, H // KV, HD)
    rotated_key_rows = reduced_precision_cast(rotate(key_pre.reshape(token_count, KV, HD), cosine, sine_tab))
    value_rows = value_rows.reshape(token_count, KV, HD)
    allowed = (segment[:, None] == segment[None, :]) & (places[None, :] <= places[:, None])
    unscaled_scores = reduced_precision_gradient(jnp.einsum('hvkq,fvq->vkhf', query_rows, rotated_key_rows, precision=lax.Precision.HIGHEST))
    scores = jnp.where(allowed, unscaled_scores * (1.0 / math.sqrt(HD)), MASKED)
    softmax_weights = reduced_precision_cast(jax.nn.softmax(scores, axis=-1))
    combined_head_output = reduced_precision_cast(reduced_precision_gradient(jnp.einsum('zpvh,hzf->vzpf', softmax_weights, value_rows, precision=lax.Precision.HIGHEST)))
    attn_out = reduced_precision_gradient(matmul(combined_head_output.reshape(token_count, H * HD), wo_full))
    residual = block_in + attn_out
    normed_mlp = reduced_precision_cast(rms_norm(residual, gain_mlp))
    gate_pre = reduced_precision_gradient(matmul(normed_mlp, wg_full))
    upward = reduced_precision_gradient(matmul(normed_mlp, wu_full))
    hidden = reduced_precision_cast(jax.nn.silu(gate_pre) * upward)
    return residual + reduced_precision_gradient(matmul(hidden, wd_full))

def reference(hidden_in, row_lengths, norm_attn, w_query, b_query, w_key, b_key, w_value, b_value, w_out, norm_mlp, w_gate, w_up, w_down, out_grad):
    params = tuple((weight.astype(jnp.float32) for weight in (norm_attn, w_query, b_query, w_key, b_key, w_value, b_value, w_out, norm_mlp, w_gate, w_up, w_down)))
    batched = hidden_in.reshape(BATCHES, BATCH, D)

    def whole_layer(params_in, inputs):

        def single(pair_in):
            return block_layer(params_in, pair_in[0], pair_in[1])
        return lax.map(jax.checkpoint(single), (inputs, row_lengths))
    outputs, pull_back = jax.vjp(whole_layer, params, batched)
    param_grads, grad_inputs = pull_back(out_grad.reshape(BATCHES, BATCH, D))
    return (outputs.reshape(TOKENS, D), grad_inputs.reshape(TOKENS, D), param_grads[0], param_grads[1], param_grads[2], param_grads[3], param_grads[4], param_grads[5], param_grads[6], param_grads[7], param_grads[8], param_grads[9], param_grads[10], param_grads[11])
```

```python
import math

import jax
import jax.numpy as jnp
from jax import lax
from jax.sharding import PartitionSpec as P

NORM_EPS = 1e-06
ROPE_BASE = 1000000.0
MASKED = -1e30


def rms_norm(value_rows, gain_vec):
    return (
        value_rows
        * lax.rsqrt(jnp.mean(value_rows * value_rows, axis=-1, keepdims=True) + NORM_EPS)
        * gain_vec
    )


def layout(lengths_row, token_count):
    row_ends = jnp.cumsum(lengths_row)
    places = jnp.arange(token_count, dtype=jnp.int32)
    passed = (places[:, None] >= row_ends[None, :]).astype(jnp.int32)
    segment = jnp.sum(passed, axis=1)
    offset = jnp.sum(passed * lengths_row[None, :], axis=1)
    return (segment, places - offset)


def rotary_tables(positions, head_dim):
    half_dim = head_dim // 2
    frequency = jnp.exp(
        jnp.arange(half_dim, dtype=jnp.float32) * (-2.0 * math.log(ROPE_BASE) / head_dim)
    )
    angles = positions.astype(jnp.float32)[:, None] * frequency[None, :]
    cosine = jnp.cos(angles)
    sine_tab = jnp.sin(angles)
    return (jnp.concatenate([cosine, cosine], -1), jnp.concatenate([sine_tab, sine_tab], -1))


def rotate(value_rows, cosine, sine_tab):
    half_dim = value_rows.shape[-1] // 2
    turned = jnp.concatenate([-value_rows[..., half_dim:], value_rows[..., :half_dim]], -1)
    return value_rows * cosine + turned * sine_tab


def unrotate(grads_in, cosine, sine_tab):
    half_dim = grads_in.shape[-1] // 2
    scaled = grads_in * sine_tab
    return grads_in * cosine + jnp.concatenate(
        [scaled[..., half_dim:], -scaled[..., :half_dim]], -1
    )


def product(left_side, right_side):
    return jnp.dot(left_side, right_side, preferred_element_type=jnp.float32)


def contract_last(left_side, right_side):
    return lax.dot_general(
        left_side, right_side, (((1,), (1,)), ((), ())), preferred_element_type=jnp.float32
    )


def contract_first(left_side, right_side):
    return lax.dot_general(
        left_side, right_side, (((0,), (0,)), ((), ())), preferred_element_type=jnp.float32
    )


def attend_forward(query_rot, key_rot, value_low, allowed):
    score_scale = 1.0 / math.sqrt(query_rot.shape[-1])
    raw = jnp.einsum("qhd,kd->hqk", query_rot, key_rot, preferred_element_type=jnp.float32)
    scores = jnp.where(allowed[None], raw * score_scale, MASKED)
    row_max = jnp.max(scores, axis=-1, keepdims=True)
    exp_scores = jnp.exp(scores - row_max)
    row_total = jnp.sum(exp_scores, axis=-1, keepdims=True)
    probs = exp_scores / row_total
    heads_out = jnp.einsum(
        "hqk,kd->qhd", probs.astype(jnp.bfloat16), value_low, preferred_element_type=jnp.float32
    )
    return (heads_out, row_max + jnp.log(row_total))


def attend_backward(query_rot, key_rot, value_low, allowed, log_sums, grad_heads):
    score_scale = 1.0 / math.sqrt(query_rot.shape[-1])
    raw = jnp.einsum("qhd,kd->hqk", query_rot, key_rot, preferred_element_type=jnp.float32)
    scores = jnp.where(allowed[None], raw * score_scale, MASKED)
    probs = jnp.exp(scores - log_sums)
    probs_low = probs.astype(jnp.bfloat16)
    value_grad = jnp.einsum(
        "hqk,qhd->kd", probs_low, grad_heads, preferred_element_type=jnp.float32
    )
    grad_probs = jnp.einsum(
        "qhd,kd->hqk", grad_heads, value_low, preferred_element_type=jnp.float32
    )
    centre = jnp.sum(grad_probs * probs, axis=-1, keepdims=True)
    grad_scores = (probs * (grad_probs - centre) * score_scale).astype(jnp.bfloat16)
    query_grad = jnp.einsum(
        "hqk,kd->qhd", grad_scores, key_rot, preferred_element_type=jnp.float32
    )
    key_grad = jnp.einsum(
        "hqk,qhd->kd", grad_scores, query_rot, preferred_element_type=jnp.float32
    )
    return (query_grad, key_grad, value_grad)


DP = ("z", "p")
POOL = ("z", "head")


def gather(x, axes):
    return lax.all_gather(x, axes, axis=0, tiled=True)


def scatter_sum(x, axes):
    return lax.psum_scatter(x.astype(jnp.bfloat16), axes, scatter_dimension=0, tiled=True)


def local(
    hidden_in,
    row_lengths,
    norm_attn,
    w_query,
    b_query,
    w_key,
    b_key,
    w_value,
    b_value,
    w_out,
    norm_mlp,
    w_gate,
    w_up,
    w_down,
    out_grad,
):
    bf = jnp.bfloat16
    quarters = lax.axis_size("z")
    plane = lax.axis_size("p")
    lanes = lax.axis_size("head")
    lane_index = lax.axis_index("head")
    shards = quarters * plane
    local_rows = hidden_in.shape[0]
    token_count = local_rows * lanes
    depth = norm_attn.shape[0]
    width = hidden_in.shape[1]
    head_dim = w_key.shape[1]
    query_width = w_query.shape[1]
    group_heads = query_width // head_dim
    hidden_width = w_gate.shape[1]
    part_width = hidden_width // quarters
    segment, positions = layout(row_lengths[0], token_count)
    cosine, sine_tab = rotary_tables(positions, head_dim)
    cosine = cosine[:, None, :]
    sine_tab = sine_tab[:, None, :]
    place = jnp.arange(token_count, dtype=jnp.int32)
    allowed = (segment[:, None] == segment[None, :]) & (place[None, :] <= place[:, None])

    attn_set = gather(jnp.concatenate([w_query, w_key, w_value, w_out.T], 1), DP)
    small = gather(
        jnp.concatenate([norm_attn, norm_mlp, b_query[0], b_key[0], b_value[0]])[None], DP
    )
    wq_full = attn_set[:, :query_width]
    wk_full = attn_set[:, query_width : query_width + head_dim]
    wv_full = attn_set[:, query_width + head_dim : query_width + 2 * head_dim]
    wo_rows = attn_set[:, query_width + 2 * head_dim :]
    cuts = [depth, depth, b_query.shape[1], b_key.shape[1], b_value.shape[1]]
    edges = [sum(cuts[:i]) for i in range(6)]
    gain_attn, gain_mlp, bias_query, bias_key, bias_value = [
        small[:, edges[i] : edges[i + 1]].reshape(-1).astype(jnp.float32) for i in range(5)
    ]

    def hidden_parts(rows):
        split = rows.reshape(depth, quarters, part_width).transpose(1, 0, 2)
        mine = lax.all_to_all(split, "z", 0, 0, tiled=True)
        return mine

    mlp_set = jnp.concatenate(
        [hidden_parts(w_gate), hidden_parts(w_up), hidden_parts(w_down.T)], -1
    )
    mlp_set = lax.all_gather(mlp_set, "p", axis=1, tiled=False).reshape(width, 3 * part_width)
    wg = mlp_set[:, :part_width]
    wu = mlp_set[:, part_width : 2 * part_width]
    wd_rows = mlp_set[:, 2 * part_width :]
    grad_rows = gather(out_grad.astype(bf), POOL)

    normed_low = gather(rms_norm(hidden_in, gain_attn).astype(bf), "head")
    query_pre = product(normed_low, wq_full) + bias_query
    key_pre = product(normed_low, wk_full) + bias_key
    value_low = (product(normed_low, wv_full) + bias_value).astype(bf)
    query_rot = rotate(
        query_pre.reshape(token_count, group_heads, head_dim), cosine, sine_tab
    ).astype(bf)
    key_rot = rotate(key_pre[:, None, :], cosine, sine_tab)[:, 0].astype(bf)
    heads_out, log_sums = attend_forward(query_rot, key_rot, value_low, allowed)
    heads_low = heads_out.reshape(token_count, query_width).astype(bf)
    residual = hidden_in + scatter_sum(contract_last(heads_low, wo_rows), "head").astype(
        jnp.float32
    )
    mlp_low = gather(rms_norm(residual, gain_mlp).astype(bf), POOL)
    gate_pre = product(mlp_low, wg)
    up_pre = product(mlp_low, wu)
    sigmoid_gate = jax.nn.sigmoid(gate_pre)
    silu_gate = gate_pre * sigmoid_gate
    hidden_low = (silu_gate * up_pre).astype(bf)
    block_out = residual + scatter_sum(contract_last(hidden_low, wd_rows), POOL).astype(
        jnp.float32
    )
    grad_hidden = product(grad_rows, wd_rows)
    grad_gate = (
        grad_hidden * up_pre * sigmoid_gate * (1.0 + gate_pre * (1.0 - sigmoid_gate))
    ).astype(bf)
    grad_up = (grad_hidden * silu_gate).astype(bf)
    grad_normed_mlp = scatter_sum(
        contract_last(grad_gate, wg) + contract_last(grad_up, wu), POOL
    ).astype(jnp.float32)
    mlp_terms = jnp.concatenate(
        [
            contract_first(mlp_low, grad_gate),
            contract_first(mlp_low, grad_up),
            contract_first(grad_rows, hidden_low),
        ],
        1,
    ).astype(bf)
    mlp_terms = mlp_terms.reshape(quarters, plane, depth, 3 * part_width).transpose(1, 0, 2, 3)
    mlp_terms = scatter_sum(mlp_terms.reshape(width, 3 * part_width), "p")
    mlp_terms = mlp_terms.reshape(quarters, depth, 3 * part_width)
    mlp_terms = lax.all_to_all(mlp_terms, "z", 0, 0, tiled=True).astype(jnp.float32)

    def whole_rows(index):
        piece = mlp_terms[:, :, index * part_width : (index + 1) * part_width]
        return piece.transpose(1, 0, 2).reshape(depth, hidden_width)

    grad_w_gate, grad_w_up = (whole_rows(0), whole_rows(1))
    grad_w_down = (
        mlp_terms[:, :, 2 * part_width :].transpose(0, 2, 1).reshape(hidden_width, depth)
    )

    _, mlp_pull = jax.vjp(rms_norm, residual, gain_mlp)
    grad_residual_part, grad_gain_mlp = mlp_pull(grad_normed_mlp)
    grad_residual = out_grad + grad_residual_part
    grad_attn_rows = gather(grad_residual.astype(bf), "head")
    grad_heads = product(grad_attn_rows, wo_rows).astype(bf)
    query_grad, key_grad, value_grad = attend_backward(
        query_rot,
        key_rot,
        value_low,
        allowed,
        log_sums,
        grad_heads.reshape(token_count, group_heads, head_dim),
    )
    grad_query = (
        unrotate(query_grad, cosine, sine_tab).reshape(token_count, query_width).astype(bf)
    )
    grad_key = unrotate(key_grad[:, None, :], cosine, sine_tab)[:, 0].astype(bf)
    grad_value = value_grad.astype(bf)
    grad_qkv = jnp.concatenate([grad_query, grad_key, grad_value], 1)
    grad_normed_attn = scatter_sum(
        contract_last(grad_qkv, attn_set[:, : query_width + 2 * head_dim]), "head"
    ).astype(jnp.float32)
    _, attn_pull = jax.vjp(rms_norm, hidden_in, gain_attn)
    grad_in_part, grad_gain_attn = attn_pull(grad_normed_attn)
    grad_in = grad_residual + grad_in_part
    attn_terms = jnp.concatenate(
        [contract_first(normed_low, grad_qkv), contract_first(grad_attn_rows, heads_low)], 1
    )
    attn_part = scatter_sum(attn_terms, DP).astype(jnp.float32)
    bias_vec = jnp.sum(grad_qkv.astype(jnp.float32), 0)
    lane_pick = (jnp.arange(lanes, dtype=jnp.int32) == lane_index).astype(jnp.float32)
    bias_rows = lane_pick[:, None] * bias_vec[None, :]
    gain_rows = jnp.stack([grad_gain_attn, grad_gain_mlp])
    gain_total, bias_total = lax.psum((gain_rows, bias_rows), ("z", "p", "head"))
    return (
        block_out,
        grad_in,
        gain_total[0],
        attn_part[:, :query_width],
        bias_total[:, :query_width],
        attn_part[:, query_width : query_width + head_dim],
        bias_total[:, query_width : query_width + head_dim],
        attn_part[:, query_width + head_dim : query_width + 2 * head_dim],
        bias_total[:, query_width + head_dim :],
        attn_part[:, query_width + 2 * head_dim :].T,
        gain_total[1],
        grad_w_gate,
        grad_w_up,
        grad_w_down,
    )


def solution(mesh):
    shards = mesh.shape["dp"]
    plane = 4 if shards % 4 == 0 else 1
    split = jax.sharding.Mesh(
        mesh.devices.reshape(shards // plane, plane, mesh.shape["head"]), ("z", "p", "head")
    )
    rows = P(("z", "p", "head"), None)
    deep = P(DP, "head")
    wide = P("head", DP)
    placed = (
        rows,
        P(DP, None),
        P(DP),
        deep,
        wide,
        deep,
        wide,
        deep,
        wide,
        wide,
        P(DP),
        deep,
        deep,
        wide,
        rows,
    )
    return jax.shard_map(
        local,
        mesh=split,
        in_specs=placed,
        out_specs=(
            rows,
            rows,
            P(),
            deep,
            P(),
            deep,
            P(),
            deep,
            P(),
            wide,
            P(),
            deep,
            deep,
            wide,
        ),
        check_vma=False,
    )
```

```python
import functools
import math

import jax
import jax.numpy as jnp
from jax import lax
from jax.experimental import pallas as pl
from jax.experimental.pallas import tpu as pltpu
from jax.sharding import PartitionSpec as P

NORM_EPS = 1e-06
ROPE_BASE = 1000000.0
MASKED = -1e30


def rms_norm(value_rows, gain_vec):
    return (
        value_rows
        * lax.rsqrt(jnp.mean(value_rows * value_rows, axis=-1, keepdims=True) + NORM_EPS)
        * gain_vec
    )


def layout(lengths_row, token_count):
    row_ends = jnp.cumsum(lengths_row)
    places = jnp.arange(token_count, dtype=jnp.int32)
    passed = (places[:, None] >= row_ends[None, :]).astype(jnp.int32)
    segment = jnp.sum(passed, axis=1)
    offset = jnp.sum(passed * lengths_row[None, :], axis=1)
    return (segment, places - offset)


def rotary_tables(positions, head_dim):
    half_dim = head_dim // 2
    frequency = jnp.exp(
        jnp.arange(half_dim, dtype=jnp.float32) * (-2.0 * math.log(ROPE_BASE) / head_dim)
    )
    angles = positions.astype(jnp.float32)[:, None] * frequency[None, :]
    cosine = jnp.cos(angles)
    sine_tab = jnp.sin(angles)
    return (jnp.concatenate([cosine, cosine], -1), jnp.concatenate([sine_tab, sine_tab], -1))


def rotate(value_rows, cosine, sine_tab):
    half_dim = value_rows.shape[-1] // 2
    turned = jnp.concatenate([-value_rows[..., half_dim:], value_rows[..., :half_dim]], -1)
    return value_rows * cosine + turned * sine_tab


def unrotate(grads_in, cosine, sine_tab):
    half_dim = grads_in.shape[-1] // 2
    scaled = grads_in * sine_tab
    return grads_in * cosine + jnp.concatenate(
        [scaled[..., half_dim:], -scaled[..., :half_dim]], -1
    )


def product(left_side, right_side):
    return jnp.dot(left_side, right_side, preferred_element_type=jnp.float32)


def contract_last(left_side, right_side):
    return lax.dot_general(
        left_side, right_side, (((1,), (1,)), ((), ())), preferred_element_type=jnp.float32
    )


def contract_first(left_side, right_side):
    return lax.dot_general(
        left_side, right_side, (((0,), (0,)), ((), ())), preferred_element_type=jnp.float32
    )


def attend_forward(query_rot, key_rot, value_low, allowed):
    score_scale = 1.0 / math.sqrt(query_rot.shape[-1])
    raw = jnp.einsum("qhd,kd->hqk", query_rot, key_rot, preferred_element_type=jnp.float32)
    scores = jnp.where(allowed[None], raw * score_scale, MASKED)
    row_max = jnp.max(scores, axis=-1, keepdims=True)
    exp_scores = jnp.exp(scores - row_max)
    row_total = jnp.sum(exp_scores, axis=-1, keepdims=True)
    probs = exp_scores / row_total
    heads_out = jnp.einsum(
        "hqk,kd->qhd", probs.astype(jnp.bfloat16), value_low, preferred_element_type=jnp.float32
    )
    return (heads_out, row_max + jnp.log(row_total))


def attend_backward(query_rot, key_rot, value_low, allowed, log_sums, grad_heads):
    score_scale = 1.0 / math.sqrt(query_rot.shape[-1])
    raw = jnp.einsum("qhd,kd->hqk", query_rot, key_rot, preferred_element_type=jnp.float32)
    scores = jnp.where(allowed[None], raw * score_scale, MASKED)
    probs = jnp.exp(scores - log_sums)
    probs_low = probs.astype(jnp.bfloat16)
    value_grad = jnp.einsum(
        "hqk,qhd->kd", probs_low, grad_heads, preferred_element_type=jnp.float32
    )
    grad_probs = jnp.einsum(
        "qhd,kd->hqk", grad_heads, value_low, preferred_element_type=jnp.float32
    )
    centre = jnp.sum(grad_probs * probs, axis=-1, keepdims=True)
    grad_scores = (probs * (grad_probs - centre) * score_scale).astype(jnp.bfloat16)
    query_grad = jnp.einsum(
        "hqk,kd->qhd", grad_scores, key_rot, preferred_element_type=jnp.float32
    )
    key_grad = jnp.einsum(
        "hqk,qhd->kd", grad_scores, query_rot, preferred_element_type=jnp.float32
    )
    return (query_grad, key_grad, value_grad)


MESH_ID = pl.DeviceIdType.MESH
PLANE = 4


def flipped(index, mask):
    bit = 1
    while bit <= mask:
        if mask & bit:
            index = index + bit - 2 * bit * lax.rem(lax.div(index, bit), 2)
        bit *= 2
    return index


def here():
    return (lax.axis_index("z"), lax.axis_index("p"), lax.axis_index("head"))


def greet(peers):
    bar = pltpu.get_barrier_semaphore()
    for peer in peers:
        pl.semaphore_signal(bar, inc=1, device_id=peer, device_id_type=MESH_ID)
    pl.semaphore_wait(bar, len(peers))


def gather_kernel(
    quarters,
    part_cols,
    aset,
    small,
    gate,
    up,
    down,
    grad,
    aset_all,
    small_all,
    gate_all,
    up_all,
    down_all,
    grad_all,
    a_send,
    a_recv,
    m_send,
    m_recv,
    s_send,
    s_recv,
    g_send,
    g_recv,
    l_sem,
):
    z, p, c = here()
    dp = z * PLANE + p
    hidden = gate.shape[1]

    def at(zz, pp):
        return (zz, pp, c)

    def send(src, dst, ssem, rsem, peer):
        copy = pltpu.make_async_remote_copy(
            src_ref=src, dst_ref=dst, send_sem=ssem, recv_sem=rsem,
            device_id=peer, device_id_type=MESH_ID,
        )
        copy.start()
        return copy

    pair = (z, p, 1 - c)
    masks = [(kz, kp) for kz in range(quarters) for kp in range(PLANE) if kz or kp]
    greet([at(flipped(z, kz), flipped(p, kp)) for kz, kp in masks] + [pair])

    def start_of(quarter):
        first = jnp.minimum(quarter * part_cols, hidden - part_cols)
        return pl.multiple_of(first, 128)

    px, py = flipped(p, 1), flipped(p, 2)
    sent = []
    arrive = {}

    def own_of(weight):
        return weight.at[:, pl.ds(start_of(z), part_cols)]

    sets = [
        (aset_all, aset, lambda zz: aset, a_send, a_recv),
        (gate_all, own_of(gate), lambda zz: gate.at[:, pl.ds(start_of(zz), part_cols)], m_send.at[0], m_recv.at[0]),
        (up_all, own_of(up), lambda zz: up.at[:, pl.ds(start_of(zz), part_cols)], m_send.at[1], m_recv.at[1]),
        (down_all, own_of(down), lambda zz: down.at[:, pl.ds(start_of(zz), part_cols)], m_send.at[2], m_recv.at[2]),
    ]

    def line(s, k):
        whole, _, part, ss, rs = sets[s]
        zz = flipped(z, k)
        sent.append(send(part(zz), whole.at[dp], ss.at[k, 0], rs.at[k, 0], at(zz, p)))

    def fan(s, k):
        whole, own, _, ss, rs = sets[s]
        slot = flipped(z, k) * PLANE + p
        src = own if k == 0 else whole.at[slot]
        if k:
            landed(s, k, 0)
        sent.append(send(src, whole.at[slot], ss.at[k, 1], rs.at[k, 1], at(z, px)))
        sent.append(send(src, whole.at[slot], ss.at[k, 2], rs.at[k, 2], at(z, py)))

    def landed(s, k, role):
        whole, _, _, ss, rs = sets[s]
        slot = flipped(z, k) * PLANE + flipped(p, role)
        pltpu.make_async_copy(whole.at[slot], whole.at[slot], rs.at[k, role]).wait()

    def relay(s, k):
        whole, _, _, ss, rs = sets[s]
        role = 1 if k % 2 == 0 else 2
        landed(s, k, role)
        slot = flipped(z, k) * PLANE + flipped(p, role)
        to = py if role == 1 else px
        sent.append(send(whole.at[slot], whole.at[slot], ss.at[k, 3], rs.at[k, 3], at(z, to)))

    def rest(s, k):
        landed(s, k, 2 if k % 2 == 0 else 1)
        landed(s, k, 3)

    for n, (kz, kp) in enumerate(masks):
        sent.append(send(small, small_all.at[dp], s_send.at[n], s_recv.at[n], at(flipped(z, kz), flipped(p, kp))))
    local = [
        pltpu.make_async_copy(small, small_all.at[dp], l_sem.at[0]),
        pltpu.make_async_copy(aset, aset_all.at[dp], l_sem.at[1]),
        pltpu.make_async_copy(sets[1][1], gate_all.at[dp], l_sem.at[2]),
        pltpu.make_async_copy(sets[2][1], up_all.at[dp], l_sem.at[3]),
        pltpu.make_async_copy(sets[3][1], down_all.at[dp], l_sem.at[4]),
        pltpu.make_async_copy(grad, grad_all.at[0, c], l_sem.at[5]),
    ]
    fan(0, 0)
    for k in range(1, quarters):
        line(0, k)
    for s in (1, 2, 3):
        for k in range(1, quarters):
            line(s, k)
    for copy in local:
        copy.start()
    sent.append(send(grad, grad_all.at[0, c], g_send.at[0, 1], g_recv.at[0, 1], pair))
    for k in range(1, quarters):
        sent.append(send(grad, grad_all.at[k, c], g_send.at[k, 0], g_recv.at[k, 0], at(flipped(z, k), p)))
    fan(1, 0)
    relay(0, 0)
    for k in range(1, quarters):
        fan(0, k)
    fan(2, 0)
    fan(3, 0)
    for k in range(1, quarters):
        relay(0, k)
    relay(1, 0)
    for k in range(1, quarters):
        fan(1, k)
    relay(2, 0)
    relay(3, 0)
    for k in range(1, quarters):
        fan(2, k)
        relay(1, k)
    for k in range(1, quarters):
        fan(3, k)
        relay(2, k)
    for k in range(1, quarters):
        relay(3, k)
    for k in range(1, quarters):
        slot = grad_all.at[k, c]
        pltpu.make_async_copy(slot, slot, g_recv.at[k, 0]).wait()
        sent.append(send(slot, slot, g_send.at[k, 1], g_recv.at[k, 1], pair))
    for k in range(quarters):
        slot = grad_all.at[k, 1 - c]
        pltpu.make_async_copy(slot, slot, g_recv.at[k, 1]).wait()
    for s in range(4):
        for k in range(quarters):
            rest(s, k)
    for n, (kz, kp) in enumerate(masks):
        slot = small_all.at[flipped(z, kz) * PLANE + flipped(p, kp)]
        pltpu.make_async_copy(slot, slot, s_recv.at[n]).wait()
    for copy in local:
        copy.wait()
    for copy in sent:
        copy.wait_send()


def gather_all(aset, small, gate, up, down, grad, shards, part_cols):
    quarters = shards // PLANE
    bf = jnp.bfloat16
    depth = aset.shape[0]
    dma = pltpu.SemaphoreType.DMA
    part = jax.ShapeDtypeStruct((shards, depth, part_cols), bf)
    return pl.pallas_call(
        functools.partial(gather_kernel, quarters, part_cols),
        out_shape=(
            jax.ShapeDtypeStruct((shards,) + aset.shape, bf),
            jax.ShapeDtypeStruct((shards,) + small.shape, bf),
            part,
            part,
            part,
            jax.ShapeDtypeStruct((quarters, 2) + grad.shape, bf),
        ),
        in_specs=[pl.BlockSpec(memory_space=pl.ANY)] * 6,
        out_specs=[pl.BlockSpec(memory_space=pl.ANY)] * 6,
        scratch_shapes=[
            dma((quarters, 4)),
            dma((quarters, 4)),
            dma((3, quarters, 4)),
            dma((3, quarters, 4)),
            dma((shards - 1,)),
            dma((shards - 1,)),
            dma((quarters, 2)),
            dma((quarters, 2)),
            dma((6,)),
        ],
        compiler_params=pltpu.CompilerParams(collective_id=0, has_side_effects=True),
    )(aset, small, gate, up, down, grad)

AHEAD = 1
LAG = 1
PARTS = (1, 2, 3, 0)
def reduce_kernel(
    quarters,
    small,
    attn,
    gate,
    up,
    down,
    small_sum,
    attn_sum,
    gate_out,
    up_out,
    down_out,
    small_all,
    attn_slots,
    mlp_slots,
    attn_line,
    staged,
    t_send,
    t_recv,
    z_send,
    z_recv,
    s_send,
    s_recv,
    l_sem,
):
    z, p, c = here()
    pair = (z, p, 1 - c)
    masks = [(kz, kp) for kz in range(quarters) for kp in range(PLANE) if kz or kp]
    greet([(flipped(z, kz), flipped(p, kp), c) for kz, kp in masks] + [pair])
    sent = []

    def send(src, dst, ssem, rsem, peer):
        copy = pltpu.make_async_remote_copy(
            src_ref=src, dst_ref=dst, send_sem=ssem, recv_sem=rsem,
            device_id=peer, device_id_type=MESH_ID,
        )
        copy.start()
        sent.append(copy)

    def landed(ref, sem):
        pltpu.make_async_copy(ref, ref, sem).wait()

    side = [(z, flipped(p, 1), c), (z, flipped(p, 2), c)]
    sources = (attn, gate, up, down)
    outs = (None, gate_out, up_out, down_out)

    def slots(s, k, role):
        return attn_slots.at[k, role] if s == 0 else mlp_slots.at[s - 1, k, role]

    def block(s, k, kp):
        return sources[s].at[flipped(z, k) * PLANE + flipped(p, kp)]

    def first(s, k):
        way = k % 2
        send(block(s, k, 3), slots(s, k, 0), t_send.at[s, k, 0], t_recv.at[s, k, 0], side[way])
        send(block(s, k, 1 + way), slots(s, k, 1), t_send.at[s, k, 1], t_recv.at[s, k, 1], side[way])

    def add(ref, other):
        total = ref[...].astype(jnp.float32) + other[...].astype(jnp.float32)
        ref[...] = total.astype(ref.dtype)

    def relay(s, k):
        way = k % 2
        slot = slots(s, k, 0)
        landed(slot, t_recv.at[s, k, 0])
        add(slot, block(s, k, 2 - way))
        send(slot, slots(s, k, 2), t_send.at[s, k, 2], t_recv.at[s, k, 2], side[1 - way])

    local = []

    def last(s, k):
        one, two = (slots(s, k, 1), slots(s, k, 2))
        landed(one, t_recv.at[s, k, 1])
        landed(two, t_recv.at[s, k, 2])
        total = (
            block(s, k, 0)[...].astype(jnp.float32)
            + one[...].astype(jnp.float32)
            + two[...].astype(jnp.float32)
        )
        one[...] = total.astype(one.dtype)
        if s == 0:
            if k:
                send(one, attn_line.at[k], z_send.at[s, k], z_recv.at[s, k], (flipped(z, k), p, c))
        elif k:
            send(one, outs[s].at[z], z_send.at[s, k], z_recv.at[s, k], (flipped(z, k), p, c))
        else:
            copy = pltpu.make_async_copy(one, outs[s].at[z], l_sem.at[s])
            copy.start()
            local.append(copy)

    dp = z * PLANE + p
    for n, (kz, kp) in enumerate(masks):
        send(small, small_all.at[dp], s_send.at[n], s_recv.at[n], (flipped(z, kz), flipped(p, kp), c))
    ks = list(range(1, quarters)) + [0]
    order = [(s, k) for i in range(0, quarters, 2) for s in PARTS for k in ks[i : i + 2]]
    for i in range(-AHEAD, len(order) + LAG):
        if 0 <= i + AHEAD < len(order):
            first(*order[i + AHEAD])
        if 0 <= i < len(order):
            relay(*order[i])
        if 0 <= i - LAG:
            last(*order[i - LAG])
    small_all[dp] = small[...]
    for n, (kz, kp) in enumerate(masks):
        slot = small_all.at[flipped(z, kz) * PLANE + flipped(p, kp)]
        landed(slot, s_recv.at[n])
    total = small_all[0]
    for i in range(1, quarters * PLANE):
        total = total + small_all[i]
    staged[...] = total
    small_sum[c] = total
    send(staged, small_sum.at[c], s_send.at[len(masks)], s_recv.at[len(masks)], pair)
    landed(small_sum.at[1 - c], s_recv.at[len(masks)])
    for k in range(1, quarters):
        landed(attn_line.at[k], z_recv.at[0, k])
    total = attn_slots[0, 1].astype(jnp.float32)
    for k in range(1, quarters):
        total = total + attn_line[k].astype(jnp.float32)
    attn_sum[...] = total
    for s in (1, 2, 3):
        for k in range(1, quarters):
            landed(outs[s].at[flipped(z, k)], z_recv.at[s, k])
    for copy in local:
        copy.wait()
    for copy in sent:
        copy.wait_send()


def reduce_all(small, attn, gate, up, down, shards):
    quarters = shards // PLANE
    bf = jnp.bfloat16
    dma = pltpu.SemaphoreType.DMA
    depth, part_cols = gate.shape[1:]
    vmem = pl.BlockSpec(memory_space=pltpu.VMEM)
    hbm = pl.BlockSpec(memory_space=pl.ANY)
    quarter_out = jax.ShapeDtypeStruct((quarters, depth, part_cols), bf)
    return pl.pallas_call(
        functools.partial(reduce_kernel, quarters),
        out_shape=(
            jax.ShapeDtypeStruct((2,) + small.shape, jnp.float32),
            jax.ShapeDtypeStruct(attn.shape[1:], jnp.float32),
            quarter_out,
            quarter_out,
            quarter_out,
        ),
        in_specs=[vmem] * 5,
        out_specs=[vmem, vmem, hbm, hbm, hbm],
        scratch_shapes=[
            pltpu.VMEM((shards,) + small.shape, jnp.float32),
            pltpu.VMEM((quarters, 3) + attn.shape[1:], bf),
            pltpu.VMEM((3, quarters, 3, depth, part_cols), bf),
            pltpu.VMEM((quarters,) + attn.shape[1:], bf),
            pltpu.VMEM(small.shape, jnp.float32),
            dma((4, quarters, 3)),
            dma((4, quarters, 3)),
            dma((4, quarters)),
            dma((4, quarters)),
            dma((shards,)),
            dma((shards,)),
            dma((4,)),
        ],
        compiler_params=pltpu.CompilerParams(
            collective_id=1, has_side_effects=True, vmem_limit_bytes=50 * 2**20
        ),
    )(small, attn, gate, up, down)


DP = ("z", "p")
POOL = ("z", "head")


def gather(x, axes):
    return lax.all_gather(x, axes, axis=0, tiled=True)


def scatter_sum(x, axes):
    return lax.psum_scatter(x.astype(jnp.bfloat16), axes, scatter_dimension=0, tiled=True)


def local(
    hidden_in,
    row_lengths,
    norm_attn,
    w_query,
    b_query,
    w_key,
    b_key,
    w_value,
    b_value,
    w_out,
    norm_mlp,
    w_gate,
    w_up,
    w_down,
    out_grad,
):
    bf = jnp.bfloat16
    quarters = lax.axis_size("z")
    lanes = lax.axis_size("head")
    lane_index = lax.axis_index("head")
    shards = quarters * PLANE
    local_rows = hidden_in.shape[0]
    token_count = local_rows * lanes
    depth = norm_attn.shape[0]
    width = hidden_in.shape[1]
    head_dim = w_key.shape[1]
    query_width = w_query.shape[1]
    group_heads = query_width // head_dim
    hidden_width = w_gate.shape[1]
    part_width = -(-hidden_width // (128 * quarters)) * 128
    quarter = lax.axis_index("z")
    first_unit = jnp.minimum(quarter * part_width, hidden_width - part_width)
    valid = first_unit + jnp.arange(part_width, dtype=jnp.int32) >= quarter * part_width
    segment, positions = layout(row_lengths[0], token_count)
    cosine, sine_tab = rotary_tables(positions, head_dim)
    cosine = cosine[:, None, :]
    sine_tab = sine_tab[:, None, :]
    place = jnp.arange(token_count, dtype=jnp.int32)
    allowed = (segment[:, None] == segment[None, :]) & (place[None, :] <= place[:, None])

    small = jnp.concatenate([norm_attn, norm_mlp, b_query[0], b_key[0], b_value[0]])
    used = small.shape[0]
    rows_used = -(-used // (128 * 16)) * 16
    small = jnp.pad(small, (0, rows_used * 128 - used)).reshape(rows_used, 128)
    attn_set, small, wg, wu, wd_rows, grad_rows = gather_all(
        jnp.concatenate([w_query, w_key, w_value, w_out.T], 1),
        small,
        w_gate,
        w_up,
        w_down.T,
        out_grad.astype(bf),
        shards,
        part_width,
    )
    attn_set = attn_set.reshape(width, attn_set.shape[2])
    small = small.reshape(shards, rows_used * 128)
    wg, wu, wd_rows = [w.reshape(width, part_width) for w in (wg, wu, wd_rows)]
    grad_rows = grad_rows[lax.bitwise_xor(jnp.arange(quarters, dtype=jnp.int32), quarter)]
    grad_rows = grad_rows.reshape(quarters * token_count, width)
    wq_full = attn_set[:, :query_width]
    wk_full = attn_set[:, query_width : query_width + head_dim]
    wv_full = attn_set[:, query_width + head_dim : query_width + 2 * head_dim]
    wo_rows = attn_set[:, query_width + 2 * head_dim :]
    cuts = [depth, depth, b_query.shape[1], b_key.shape[1], b_value.shape[1]]
    edges = [sum(cuts[:i]) for i in range(6)]
    gain_attn, gain_mlp, bias_query, bias_key, bias_value = [
        small[:, edges[i] : edges[i + 1]].reshape(-1).astype(jnp.float32) for i in range(5)
    ]

    normed_low = gather(rms_norm(hidden_in, gain_attn).astype(bf), "head")
    query_pre = product(normed_low, wq_full) + bias_query
    key_pre = product(normed_low, wk_full) + bias_key
    value_low = (product(normed_low, wv_full) + bias_value).astype(bf)
    query_rot = rotate(
        query_pre.reshape(token_count, group_heads, head_dim), cosine, sine_tab
    ).astype(bf)
    key_rot = rotate(key_pre[:, None, :], cosine, sine_tab)[:, 0].astype(bf)
    heads_out, log_sums = attend_forward(query_rot, key_rot, value_low, allowed)
    heads_low = heads_out.reshape(token_count, query_width).astype(bf)
    residual = hidden_in + scatter_sum(contract_last(heads_low, wo_rows), "head").astype(
        jnp.float32
    )
    mlp_low = gather(rms_norm(residual, gain_mlp).astype(bf), POOL)
    gate_pre = jnp.where(valid, product(mlp_low, wg), 0.0)
    up_pre = jnp.where(valid, product(mlp_low, wu), 0.0)
    sigmoid_gate = jax.nn.sigmoid(gate_pre)
    silu_gate = gate_pre * sigmoid_gate
    hidden_low = (silu_gate * up_pre).astype(bf)
    block_out = residual + scatter_sum(contract_last(hidden_low, wd_rows), POOL).astype(
        jnp.float32
    )
    grad_hidden = product(grad_rows, wd_rows)
    grad_gate = (
        grad_hidden * up_pre * sigmoid_gate * (1.0 + gate_pre * (1.0 - sigmoid_gate))
    ).astype(bf)
    grad_up = (grad_hidden * silu_gate).astype(bf)
    grad_normed_mlp = scatter_sum(
        contract_last(grad_gate, wg) + contract_last(grad_up, wu), POOL
    ).astype(jnp.float32)
    mlp_terms = [
        contract_first(left, right).astype(bf).reshape(shards, depth, part_width)
        for left, right in (
            (mlp_low, grad_gate),
            (mlp_low, grad_up),
            (grad_rows, hidden_low),
        )
    ]

    _, mlp_pull = jax.vjp(rms_norm, residual, gain_mlp)
    grad_residual_part, grad_gain_mlp = mlp_pull(grad_normed_mlp)
    grad_residual = out_grad + grad_residual_part
    grad_attn_rows = gather(grad_residual.astype(bf), "head")
    grad_heads = product(grad_attn_rows, wo_rows).astype(bf)
    query_grad, key_grad, value_grad = attend_backward(
        query_rot,
        key_rot,
        value_low,
        allowed,
        log_sums,
        grad_heads.reshape(token_count, group_heads, head_dim),
    )
    grad_query = (
        unrotate(query_grad, cosine, sine_tab).reshape(token_count, query_width).astype(bf)
    )
    grad_key = unrotate(key_grad[:, None, :], cosine, sine_tab)[:, 0].astype(bf)
    grad_value = value_grad.astype(bf)
    grad_qkv = jnp.concatenate([grad_query, grad_key, grad_value], 1)
    grad_normed_attn = scatter_sum(
        contract_last(grad_qkv, attn_set[:, : query_width + 2 * head_dim]), "head"
    ).astype(jnp.float32)
    _, attn_pull = jax.vjp(rms_norm, hidden_in, gain_attn)
    grad_in_part, grad_gain_attn = attn_pull(grad_normed_attn)
    grad_in = grad_residual + grad_in_part
    attn_terms = jnp.concatenate(
        [contract_first(normed_low, grad_qkv), contract_first(grad_attn_rows, heads_low)], 1
    )
    bias_vec = jnp.sum(grad_qkv.astype(jnp.float32), 0)
    small_grads = jnp.concatenate([grad_gain_attn, grad_gain_mlp, bias_vec]).reshape(-1, 128)
    small_total, attn_part, *quarter_grads = reduce_all(
        small_grads,
        attn_terms.astype(bf).reshape(shards, depth, attn_terms.shape[1]),
        *mlp_terms,
        shards,
    )
    small_total = small_total.reshape(lanes, -1)
    gain_total = jnp.sum(small_total[:, : 2 * width], 0).reshape(2, width)
    bias_total = small_total[:, 2 * width :]

    def whole_rows(parts):
        taken = []
        for index in range(quarters):
            skip = max(0, index * part_width - (hidden_width - part_width))
            if skip < part_width:
                taken.append(parts[index][:, skip:])
        return jnp.concatenate(taken, 1).astype(jnp.float32)

    grad_w_gate, grad_w_up, grad_w_down = [whole_rows(parts) for parts in quarter_grads]
    grad_w_down = grad_w_down.T
    return (
        block_out,
        grad_in,
        gain_total[0],
        attn_part[:, :query_width],
        bias_total[:, :query_width],
        attn_part[:, query_width : query_width + head_dim],
        bias_total[:, query_width : query_width + head_dim],
        attn_part[:, query_width + head_dim : query_width + 2 * head_dim],
        bias_total[:, query_width + head_dim :],
        attn_part[:, query_width + 2 * head_dim :].T,
        gain_total[1],
        grad_w_gate,
        grad_w_up,
        grad_w_down,
    )


def solution(mesh):
    shards = mesh.shape["dp"]
    plane = 4 if shards % 4 == 0 else 1
    split = jax.sharding.Mesh(
        mesh.devices.reshape(shards // plane, plane, mesh.shape["head"]), ("z", "p", "head")
    )
    rows = P(("z", "p", "head"), None)
    deep = P(DP, "head")
    wide = P("head", DP)
    placed = (
        rows,
        P(DP, None),
        P(DP),
        deep,
        wide,
        deep,
        wide,
        deep,
        wide,
        wide,
        P(DP),
        deep,
        deep,
        wide,
        rows,
    )
    return jax.shard_map(
        local,
        mesh=split,
        in_specs=placed,
        out_specs=(
            rows,
            rows,
            P(),
            deep,
            P(),
            deep,
            P(),
            deep,
            P(),
            wide,
            P(),
            deep,
            deep,
            wide,
        ),
        check_vma=False,
    )
```

```python
import functools
import math

import jax
import jax.numpy as jnp
from jax import lax
from jax.experimental import pallas as pl
from jax.experimental.pallas import tpu as pltpu
from jax.sharding import PartitionSpec as P

NORM_EPS = 1e-06
ROPE_BASE = 1000000.0
MASKED = -1e30


def rms_norm(value_rows, gain_vec):
    return (
        value_rows
        * lax.rsqrt(jnp.mean(value_rows * value_rows, axis=-1, keepdims=True) + NORM_EPS)
        * gain_vec
    )


def layout(lengths_row, token_count):
    row_ends = jnp.cumsum(lengths_row)
    places = jnp.arange(token_count, dtype=jnp.int32)
    passed = (places[:, None] >= row_ends[None, :]).astype(jnp.int32)
    segment = jnp.sum(passed, axis=1)
    offset = jnp.sum(passed * lengths_row[None, :], axis=1)
    return (segment, places - offset)


def rotary_tables(positions, head_dim):
    half_dim = head_dim // 2
    frequency = jnp.exp(
        jnp.arange(half_dim, dtype=jnp.float32) * (-2.0 * math.log(ROPE_BASE) / head_dim)
    )
    angles = positions.astype(jnp.float32)[:, None] * frequency[None, :]
    cosine = jnp.cos(angles)
    sine_tab = jnp.sin(angles)
    return (jnp.concatenate([cosine, cosine], -1), jnp.concatenate([sine_tab, sine_tab], -1))


def rotate(value_rows, cosine, sine_tab):
    half_dim = value_rows.shape[-1] // 2
    turned = jnp.concatenate([-value_rows[..., half_dim:], value_rows[..., :half_dim]], -1)
    return value_rows * cosine + turned * sine_tab


def unrotate(grads_in, cosine, sine_tab):
    half_dim = grads_in.shape[-1] // 2
    scaled = grads_in * sine_tab
    return grads_in * cosine + jnp.concatenate(
        [scaled[..., half_dim:], -scaled[..., :half_dim]], -1
    )


def product(left_side, right_side):
    return jnp.dot(left_side, right_side, preferred_element_type=jnp.float32)


def contract_last(left_side, right_side):
    return lax.dot_general(
        left_side, right_side, (((1,), (1,)), ((), ())), preferred_element_type=jnp.float32
    )


def contract_first(left_side, right_side):
    return lax.dot_general(
        left_side, right_side, (((0,), (0,)), ((), ())), preferred_element_type=jnp.float32
    )


def attend_forward(query_rot, key_rot, value_low, allowed):
    score_scale = 1.0 / math.sqrt(query_rot.shape[-1])
    raw = jnp.einsum("qhd,kd->hqk", query_rot, key_rot, preferred_element_type=jnp.float32)
    scores = jnp.where(allowed[None], raw * score_scale, MASKED)
    row_max = jnp.max(scores, axis=-1, keepdims=True)
    exp_scores = jnp.exp(scores - row_max)
    row_total = jnp.sum(exp_scores, axis=-1, keepdims=True)
    probs = exp_scores / row_total
    heads_out = jnp.einsum(
        "hqk,kd->qhd", probs.astype(jnp.bfloat16), value_low, preferred_element_type=jnp.float32
    )
    return (heads_out, row_max + jnp.log(row_total))


def attend_backward(query_rot, key_rot, value_low, allowed, log_sums, grad_heads):
    score_scale = 1.0 / math.sqrt(query_rot.shape[-1])
    raw = jnp.einsum("qhd,kd->hqk", query_rot, key_rot, preferred_element_type=jnp.float32)
    scores = jnp.where(allowed[None], raw * score_scale, MASKED)
    probs = jnp.exp(scores - log_sums)
    probs_low = probs.astype(jnp.bfloat16)
    value_grad = jnp.einsum(
        "hqk,qhd->kd", probs_low, grad_heads, preferred_element_type=jnp.float32
    )
    grad_probs = jnp.einsum(
        "qhd,kd->hqk", grad_heads, value_low, preferred_element_type=jnp.float32
    )
    centre = jnp.sum(grad_probs * probs, axis=-1, keepdims=True)
    grad_scores = (probs * (grad_probs - centre) * score_scale).astype(jnp.bfloat16)
    query_grad = jnp.einsum(
        "hqk,kd->qhd", grad_scores, key_rot, preferred_element_type=jnp.float32
    )
    key_grad = jnp.einsum(
        "hqk,qhd->kd", grad_scores, query_rot, preferred_element_type=jnp.float32
    )
    return (query_grad, key_grad, value_grad)


MESH_ID = pl.DeviceIdType.MESH
PLANE = 4


def flipped(index, mask):
    bit = 1
    while bit <= mask:
        if mask & bit:
            index = index + bit - 2 * bit * lax.rem(lax.div(index, bit), 2)
        bit *= 2
    return index


def spot(z, p, c):
    return {"z": z, "p": p, "head": c}


def here():
    return (lax.axis_index("z"), lax.axis_index("p"), lax.axis_index("head"))


def greet(peers):
    bar = pltpu.get_barrier_semaphore()
    for peer in peers:
        pl.semaphore_signal(bar, inc=1, device_id=peer, device_id_type=MESH_ID)
    pl.semaphore_wait(bar, len(peers))


def gather_kernel(
    quarters,
    part_cols,
    aset,
    small,
    gate,
    up,
    down,
    grad,
    aset_all,
    small_all,
    gate_all,
    up_all,
    down_all,
    grad_all,
    a_send,
    a_recv,
    m_send,
    m_recv,
    s_send,
    s_recv,
    g_send,
    g_recv,
    l_sem,
):
    z, p, c = here()
    dp = z * PLANE + p
    hidden = gate.shape[1]

    def at(zz, pp):
        return spot(zz, pp, c)

    def send(src, dst, ssem, rsem, peer):
        copy = pltpu.make_async_remote_copy(
            src_ref=src, dst_ref=dst, send_sem=ssem, recv_sem=rsem,
            device_id=peer, device_id_type=MESH_ID,
        )
        copy.start()
        return copy

    pair = spot(z, p, 1 - c)
    masks = [(kz, kp) for kz in range(quarters) for kp in range(PLANE) if kz or kp]
    greet([at(flipped(z, kz), flipped(p, kp)) for kz, kp in masks] + [pair])

    def start_of(quarter):
        first = jnp.minimum(quarter * part_cols, hidden - part_cols)
        return pl.multiple_of(first, 128)

    px, py = flipped(p, 1), flipped(p, 2)
    sent = []
    arrive = {}

    def own_of(weight):
        return weight.at[:, pl.ds(start_of(z), part_cols)]

    sets = [
        (aset_all, aset, lambda zz: aset, a_send, a_recv),
        (gate_all, own_of(gate), lambda zz: gate.at[:, pl.ds(start_of(zz), part_cols)], m_send.at[0], m_recv.at[0]),
        (up_all, own_of(up), lambda zz: up.at[:, pl.ds(start_of(zz), part_cols)], m_send.at[1], m_recv.at[1]),
        (down_all, own_of(down), lambda zz: down.at[:, pl.ds(start_of(zz), part_cols)], m_send.at[2], m_recv.at[2]),
    ]

    def line(s, k):
        whole, _, part, ss, rs = sets[s]
        zz = flipped(z, k)
        sent.append(send(part(zz), whole.at[dp], ss.at[k, 0], rs.at[k, 0], at(zz, p)))

    def fan(s, k):
        whole, own, _, ss, rs = sets[s]
        slot = flipped(z, k) * PLANE + p
        src = own if k == 0 else whole.at[slot]
        if k:
            landed(s, k, 0)
        sent.append(send(src, whole.at[slot], ss.at[k, 1], rs.at[k, 1], at(z, px)))
        sent.append(send(src, whole.at[slot], ss.at[k, 2], rs.at[k, 2], at(z, py)))

    def landed(s, k, role):
        whole, _, _, ss, rs = sets[s]
        slot = flipped(z, k) * PLANE + flipped(p, role)
        pltpu.make_async_copy(whole.at[slot], whole.at[slot], rs.at[k, role]).wait()

    def relay(s, k):
        whole, _, _, ss, rs = sets[s]
        role = 1 if k % 2 == 0 else 2
        landed(s, k, role)
        slot = flipped(z, k) * PLANE + flipped(p, role)
        to = py if role == 1 else px
        sent.append(send(whole.at[slot], whole.at[slot], ss.at[k, 3], rs.at[k, 3], at(z, to)))

    def rest(s, k):
        landed(s, k, 2 if k % 2 == 0 else 1)
        landed(s, k, 3)

    for n, (kz, kp) in enumerate(masks):
        sent.append(send(small, small_all.at[dp], s_send.at[n], s_recv.at[n], at(flipped(z, kz), flipped(p, kp))))
    local = [
        pltpu.make_async_copy(small, small_all.at[dp], l_sem.at[0]),
        pltpu.make_async_copy(aset, aset_all.at[dp], l_sem.at[1]),
        pltpu.make_async_copy(sets[1][1], gate_all.at[dp], l_sem.at[2]),
        pltpu.make_async_copy(sets[2][1], up_all.at[dp], l_sem.at[3]),
        pltpu.make_async_copy(sets[3][1], down_all.at[dp], l_sem.at[4]),
        pltpu.make_async_copy(grad, grad_all.at[0, c], l_sem.at[5]),
    ]
    fan(0, 0)
    for k in range(1, quarters):
        line(0, k)
    for s in (1, 2, 3):
        for k in range(1, quarters):
            line(s, k)
    for copy in local:
        copy.start()
    sent.append(send(grad, grad_all.at[0, c], g_send.at[0, 1], g_recv.at[0, 1], pair))
    for k in range(1, quarters):
        sent.append(send(grad, grad_all.at[k, c], g_send.at[k, 0], g_recv.at[k, 0], at(flipped(z, k), p)))
    fan(1, 0)
    relay(0, 0)
    for k in range(1, quarters):
        fan(0, k)
    fan(2, 0)
    fan(3, 0)
    for k in range(1, quarters):
        relay(0, k)
    relay(1, 0)
    for k in range(1, quarters):
        fan(1, k)
    relay(2, 0)
    relay(3, 0)
    for k in range(1, quarters):
        fan(2, k)
        relay(1, k)
    for k in range(1, quarters):
        fan(3, k)
        relay(2, k)
    for k in range(1, quarters):
        relay(3, k)
    for k in range(1, quarters):
        slot = grad_all.at[k, c]
        pltpu.make_async_copy(slot, slot, g_recv.at[k, 0]).wait()
        sent.append(send(slot, slot, g_send.at[k, 1], g_recv.at[k, 1], pair))
    for k in range(quarters):
        slot = grad_all.at[k, 1 - c]
        pltpu.make_async_copy(slot, slot, g_recv.at[k, 1]).wait()
    for s in range(4):
        for k in range(quarters):
            rest(s, k)
    for n, (kz, kp) in enumerate(masks):
        slot = small_all.at[flipped(z, kz) * PLANE + flipped(p, kp)]
        pltpu.make_async_copy(slot, slot, s_recv.at[n]).wait()
    for copy in local:
        copy.wait()
    for copy in sent:
        copy.wait_send()


def gather_all(aset, small, gate, up, down, grad, shards, part_cols):
    quarters = shards // PLANE
    bf = jnp.bfloat16
    depth = aset.shape[0]
    dma = pltpu.SemaphoreType.DMA
    part = jax.ShapeDtypeStruct((shards, depth, part_cols), bf)
    return pl.pallas_call(
        functools.partial(gather_kernel, quarters, part_cols),
        out_shape=(
            jax.ShapeDtypeStruct((shards,) + aset.shape, bf),
            jax.ShapeDtypeStruct((shards,) + small.shape, bf),
            part,
            part,
            part,
            jax.ShapeDtypeStruct((quarters, 2) + grad.shape, bf),
        ),
        in_specs=[pl.BlockSpec(memory_space=pl.ANY)] * 6,
        out_specs=[pl.BlockSpec(memory_space=pl.ANY)] * 6,
        scratch_shapes=[
            dma((quarters, 4)),
            dma((quarters, 4)),
            dma((3, quarters, 4)),
            dma((3, quarters, 4)),
            dma((shards - 1,)),
            dma((shards - 1,)),
            dma((quarters, 2)),
            dma((quarters, 2)),
            dma((6,)),
        ],
        compiler_params=pltpu.CompilerParams(collective_id=0, has_side_effects=True),
    )(aset, small, gate, up, down, grad)


TILE = 256


def mlp_kernel(
    quarters,
    hidden,
    own,
    grads,
    gate,
    up,
    down,
    y_out,
    d_out,
    gate_out,
    up_out,
    down_out,
    h_all,
    g_all,
    w_all,
    act,
    d_gate,
    d_up,
    y_part,
    d_part,
    y_slot,
    d_slot,
    d_line,
    h_send,
    h_recv,
    hp_send,
    hp_recv,
    y_send,
    y_recv,
    d_send,
    d_recv,
    l_send,
    l_recv,
    load_sem,
    out_sem,
):
    z, p, c = here()
    pair = spot(z, p, 1 - c)
    rows, width = own.shape
    part_cols = gate.shape[1]
    padded = w_all.shape[2]
    tiles = padded // TILE

    def moved(k):
        total, bit = 0, 1
        while bit < quarters:
            a, b = lax.rem(lax.div(z, bit), 2), lax.rem(lax.div(k, bit), 2)
            total = total + bit * (a + b - 2 * a * b)
            bit *= 2
        return total

    def send(src, dst, ssem, rsem, peer):
        pltpu.make_async_remote_copy(
            src_ref=src, dst_ref=dst, send_sem=ssem, recv_sem=rsem,
            device_id=peer, device_id_type=MESH_ID,
        ).start()

    def landed(ref, sem):
        pltpu.make_async_copy(ref, ref, sem).wait()

    def half(k, lane):
        return h_all.at[k, pl.ds(pl.multiple_of(lane * rows, 16), rows)]

    loads = [
        pltpu.make_async_copy(w, w_all.at[i, :, pl.ds(0, part_cols)], load_sem.at[i])
        for i, w in enumerate((gate, up, down))
    ] + [pltpu.make_async_copy(grads, g_all, load_sem.at[3]), pltpu.make_async_copy(own, half(0, c), load_sem.at[4])]
    for copy in loads:
        copy.start()
    greet([spot(flipped(z, k), p, c) for k in range(1, quarters)] + [pair])
    send(own, half(0, c), hp_send.at[0], hp_recv.at[0], pair)
    for k in range(1, quarters):
        send(own, half(k, c), h_send.at[k], h_recv.at[k], spot(flipped(z, k), p, c))
    if padded > part_cols:
        for i in range(3):
            w_all[i, :, part_cols:] = jnp.zeros((width, padded - part_cols), w_all.dtype)
    first = jnp.minimum(z * part_cols, hidden - part_cols)
    skip = z * part_cols - first
    for copy in loads:
        copy.wait()

    def finish(k):
        mine, other = (y_part.at[k, c], y_slot.at[k])
        landed(other, y_recv.at[k])
        other[...] = (other[...].astype(jnp.float32) + mine[...].astype(jnp.float32)).astype(other.dtype)
        pltpu.make_async_copy(other, y_out.at[k], out_sem.at[0, k]).start()
        mine, other = (d_part.at[k, c], d_slot.at[k])
        landed(other, d_recv.at[k])
        other[...] = (other[...].astype(jnp.float32) + mine[...].astype(jnp.float32)).astype(other.dtype)

        @pl.when(k > 0)
        def _():
            send(other, d_line.at[k], l_send.at[k], l_recv.at[k], spot(moved(k), p, c))

    def block(k, carry):
        @pl.when(k > 0)
        def _():
            landed(half(k, c), h_recv.at[k])
            send(half(k, c), half(k, c), hp_send.at[k], hp_recv.at[k], pair)

        landed(half(k, 1 - c), hp_recv.at[k])

        def units(n, carry):
            cols = pl.ds(pl.multiple_of(n * TILE, TILE), TILE)
            h = h_all[k]
            g = jnp.dot(h, w_all[0, :, cols], preferred_element_type=jnp.float32)
            u = jnp.dot(h, w_all[1, :, cols], preferred_element_type=jnp.float32)
            da = jnp.dot(g_all[k], w_all[2, :, cols], preferred_element_type=jnp.float32)
            column = n * TILE + lax.broadcasted_iota(jnp.int32, (1, TILE), 1)
            ok = column >= skip
            g = jnp.where(ok, g, 0.0)
            u = jnp.where(ok, u, 0.0)
            s = 1.0 / (1.0 + jnp.exp(-g))
            sg = g * s
            act[k, :, cols] = (sg * u).astype(act.dtype)
            d_gate[k, :, cols] = (da * u * s * (1.0 + g * (1.0 - s))).astype(act.dtype)
            d_up[k, :, cols] = (da * sg).astype(act.dtype)
            return carry

        lax.fori_loop(0, tiles, units, 0)

        @pl.when(k > 0)
        def _():
            finish(k - 1)

        def model(n, carry):
            cols = pl.ds(pl.multiple_of(n * TILE, TILE), TILE)

            def back(left, index):
                return lax.dot_general(
                    left[k], w_all[index, cols, :], (((1,), (1,)), ((), ())),
                    preferred_element_type=jnp.float32,
                )

            y = back(act, 2).astype(act.dtype)
            d = (back(d_gate, 0) + back(d_up, 1)).astype(act.dtype)
            for lane in range(2):
                y_part[k, lane, :, cols] = y[lane * rows : (lane + 1) * rows]
                d_part[k, lane, :, cols] = d[lane * rows : (lane + 1) * rows]
            return carry

        lax.fori_loop(0, width // TILE, model, 0)
        send(y_part.at[k, 1 - c], y_slot.at[k], y_send.at[k], y_recv.at[k], pair)
        send(d_part.at[k, 1 - c], d_slot.at[k], d_send.at[k], d_recv.at[k], pair)
        return carry

    lax.fori_loop(0, quarters, block, 0)
    finish(quarters - 1)

    outs = (gate_out, up_out, down_out)

    def weight(n, carry):
        cols = pl.ds(pl.multiple_of(n * TILE, TILE), TILE)
        for i, (left, right) in enumerate(((h_all, d_gate), (h_all, d_up), (g_all, act))):
            total = None
            for k in range(quarters):
                term = lax.dot_general(
                    left[k, :, cols], right[k], (((0,), (0,)), ((), ())),
                    preferred_element_type=jnp.float32,
                )
                total = term if total is None else total + term
            w_all[i, cols, :] = total.astype(act.dtype)
            pltpu.make_async_copy(
                w_all.at[i, cols, pl.ds(0, part_cols)], outs[i].at[cols, :], out_sem.at[1 + i, n]
            ).start()
        return carry

    lax.fori_loop(0, width // TILE, weight, 0)
    total = d_slot[0].astype(jnp.float32)
    for k in range(1, quarters):
        landed(d_line.at[k], l_recv.at[k])
        total = total + d_line[k].astype(jnp.float32)
    d_out[...] = total
    for n in range(width // TILE):
        for i in range(3):
            tile = w_all.at[i, pl.ds(n * TILE, TILE), pl.ds(0, part_cols)]
            pltpu.make_async_copy(tile, outs[i].at[pl.ds(n * TILE, TILE), :], out_sem.at[1 + i, n]).wait()
    for k in range(quarters):
        pltpu.make_async_copy(y_slot.at[k], y_out.at[k], out_sem.at[0, k]).wait()
        landed(half(k, c), hp_send.at[k])
        landed(y_part.at[k, 1 - c], y_send.at[k])
        landed(d_part.at[k, 1 - c], d_send.at[k])
        if k:
            landed(own, h_send.at[k])
            landed(d_slot.at[k], l_send.at[k])


def mlp_all(own, grads, gate, up, down, hidden):
    bf = jnp.bfloat16
    quarters, block_rows, width = grads.shape
    part_cols = gate.shape[1]
    padded = -(-part_cols // TILE) * TILE
    rows = own.shape[0]
    dma = pltpu.SemaphoreType.DMA
    hbm = pl.BlockSpec(memory_space=pl.ANY)
    vmem = pl.BlockSpec(memory_space=pltpu.VMEM)
    grad_w = jax.ShapeDtypeStruct((width, part_cols), bf)
    steps = max(quarters, width // TILE)
    return pl.pallas_call(
        functools.partial(mlp_kernel, quarters, hidden),
        out_shape=(
            jax.ShapeDtypeStruct((quarters, rows, width), bf),
            jax.ShapeDtypeStruct((rows, width), jnp.float32),
            grad_w,
            grad_w,
            grad_w,
        ),
        in_specs=[hbm] * 5,
        out_specs=[hbm, vmem, hbm, hbm, hbm],
        scratch_shapes=[
            pltpu.VMEM((quarters, block_rows, width), bf),
            pltpu.VMEM((quarters, block_rows, width), bf),
            pltpu.VMEM((3, width, padded), bf),
            pltpu.VMEM((quarters, block_rows, padded), bf),
            pltpu.VMEM((quarters, block_rows, padded), bf),
            pltpu.VMEM((quarters, block_rows, padded), bf),
            pltpu.VMEM((quarters, 2, rows, width), bf),
            pltpu.VMEM((quarters, 2, rows, width), bf),
            pltpu.VMEM((quarters, rows, width), bf),
            pltpu.VMEM((quarters, rows, width), bf),
            pltpu.VMEM((quarters, rows, width), bf),
        ]
        + [dma((quarters,))] * 10
        + [dma((5,)), dma((4, steps))],
        compiler_params=pltpu.CompilerParams(
            collective_id=2, has_side_effects=True, vmem_limit_bytes=60 * 2**20
        ),
    )(own, grads, gate, up, down)

AHEAD = 1
LAG = 1
PARTS = (1, 2, 3, 0)
def reduce_kernel(
    quarters,
    small,
    attn,
    gate,
    up,
    down,
    y_half,
    small_sum,
    attn_sum,
    y_sum,
    gate_out,
    up_out,
    down_out,
    small_all,
    attn_slots,
    mlp_slots,
    attn_line,
    y_line,
    staged,
    t_send,
    t_recv,
    z_send,
    z_recv,
    s_send,
    s_recv,
    y_send,
    y_recv,
    l_sem,
):
    z, p, c = here()
    pair = spot(z, p, 1 - c)
    masks = [(kz, kp) for kz in range(quarters) for kp in range(PLANE) if kz or kp]
    greet([spot(flipped(z, kz), flipped(p, kp), c) for kz, kp in masks] + [pair])
    sent = []

    def send(src, dst, ssem, rsem, peer):
        copy = pltpu.make_async_remote_copy(
            src_ref=src, dst_ref=dst, send_sem=ssem, recv_sem=rsem,
            device_id=peer, device_id_type=MESH_ID,
        )
        copy.start()
        sent.append(copy)

    def landed(ref, sem):
        pltpu.make_async_copy(ref, ref, sem).wait()

    side = [spot(z, flipped(p, 1), c), spot(z, flipped(p, 2), c)]
    sources = (attn, gate, up, down)
    outs = (None, gate_out, up_out, down_out)

    def slots(s, k, role):
        return attn_slots.at[k, role] if s == 0 else mlp_slots.at[s - 1, k, role]

    def block(s, k, kp):
        return sources[s].at[flipped(z, k) * PLANE + flipped(p, kp)]

    def first(s, k):
        way = k % 2
        send(block(s, k, 3), slots(s, k, 0), t_send.at[s, k, 0], t_recv.at[s, k, 0], side[way])
        send(block(s, k, 1 + way), slots(s, k, 1), t_send.at[s, k, 1], t_recv.at[s, k, 1], side[way])

    def add(ref, other):
        total = ref[...].astype(jnp.float32) + other[...].astype(jnp.float32)
        ref[...] = total.astype(ref.dtype)

    def relay(s, k):
        way = k % 2
        slot = slots(s, k, 0)
        landed(slot, t_recv.at[s, k, 0])
        add(slot, block(s, k, 2 - way))
        send(slot, slots(s, k, 2), t_send.at[s, k, 2], t_recv.at[s, k, 2], side[1 - way])

    local = []

    def last(s, k):
        one, two = (slots(s, k, 1), slots(s, k, 2))
        landed(one, t_recv.at[s, k, 1])
        landed(two, t_recv.at[s, k, 2])
        total = (
            block(s, k, 0)[...].astype(jnp.float32)
            + one[...].astype(jnp.float32)
            + two[...].astype(jnp.float32)
        )
        one[...] = total.astype(one.dtype)
        if s == 0:
            if k:
                send(one, attn_line.at[k], z_send.at[s, k], z_recv.at[s, k], spot(flipped(z, k), p, c))
        elif k:
            send(one, outs[s].at[z], z_send.at[s, k], z_recv.at[s, k], spot(flipped(z, k), p, c))
        else:
            copy = pltpu.make_async_copy(one, outs[s].at[z], l_sem.at[s])
            copy.start()
            local.append(copy)

    dp = z * PLANE + p
    for n, (kz, kp) in enumerate(masks):
        send(small, small_all.at[dp], s_send.at[n], s_recv.at[n], spot(flipped(z, kz), flipped(p, kp), c))
    for k in range(1, quarters):
        send(y_half.at[k], y_line.at[k], y_send.at[k], y_recv.at[k], spot(flipped(z, k), p, c))
    ks = list(range(1, quarters)) + [0]
    order = [(s, k) for i in range(0, quarters, 2) for s in PARTS for k in ks[i : i + 2]]
    for i in range(-AHEAD, len(order) + LAG):
        if 0 <= i + AHEAD < len(order):
            first(*order[i + AHEAD])
        if 0 <= i < len(order):
            relay(*order[i])
        if 0 <= i - LAG:
            last(*order[i - LAG])
    small_all[dp] = small[...]
    for n, (kz, kp) in enumerate(masks):
        slot = small_all.at[flipped(z, kz) * PLANE + flipped(p, kp)]
        landed(slot, s_recv.at[n])
    total = small_all[0]
    for i in range(1, quarters * PLANE):
        total = total + small_all[i]
    staged[...] = total
    small_sum[c] = total
    send(staged, small_sum.at[c], s_send.at[len(masks)], s_recv.at[len(masks)], pair)
    landed(small_sum.at[1 - c], s_recv.at[len(masks)])
    for k in range(1, quarters):
        landed(attn_line.at[k], z_recv.at[0, k])
    total = attn_slots[0, 1].astype(jnp.float32)
    for k in range(1, quarters):
        total = total + attn_line[k].astype(jnp.float32)
    attn_sum[...] = total
    total = y_half[0].astype(jnp.float32)
    for k in range(1, quarters):
        landed(y_line.at[k], y_recv.at[k])
        total = total + y_line[k].astype(jnp.float32)
    y_sum[...] = total
    for s in (1, 2, 3):
        for k in range(1, quarters):
            landed(outs[s].at[flipped(z, k)], z_recv.at[s, k])
    for copy in local:
        copy.wait()
    for copy in sent:
        copy.wait_send()


def reduce_all(small, attn, gate, up, down, y_half, shards):
    quarters = shards // PLANE
    bf = jnp.bfloat16
    dma = pltpu.SemaphoreType.DMA
    depth, part_cols = gate.shape[1:]
    vmem = pl.BlockSpec(memory_space=pltpu.VMEM)
    hbm = pl.BlockSpec(memory_space=pl.ANY)
    quarter_out = jax.ShapeDtypeStruct((quarters, depth, part_cols), bf)
    return pl.pallas_call(
        functools.partial(reduce_kernel, quarters),
        out_shape=(
            jax.ShapeDtypeStruct((2,) + small.shape, jnp.float32),
            jax.ShapeDtypeStruct(attn.shape[1:], jnp.float32),
            jax.ShapeDtypeStruct(y_half.shape[1:], jnp.float32),
            quarter_out,
            quarter_out,
            quarter_out,
        ),
        in_specs=[vmem] * 6,
        out_specs=[vmem, vmem, vmem, hbm, hbm, hbm],
        scratch_shapes=[
            pltpu.VMEM((shards,) + small.shape, jnp.float32),
            pltpu.VMEM((quarters, 3) + attn.shape[1:], bf),
            pltpu.VMEM((3, quarters, 3, depth, part_cols), bf),
            pltpu.VMEM((quarters,) + attn.shape[1:], bf),
            pltpu.VMEM(y_half.shape, bf),
            pltpu.VMEM(small.shape, jnp.float32),
            dma((4, quarters, 3)),
            dma((4, quarters, 3)),
            dma((4, quarters)),
            dma((4, quarters)),
            dma((shards,)),
            dma((shards,)),
            dma((quarters,)),
            dma((quarters,)),
            dma((4,)),
        ],
        compiler_params=pltpu.CompilerParams(
            collective_id=1, has_side_effects=True, vmem_limit_bytes=50 * 2**20
        ),
    )(small, attn, gate, up, down, y_half)


DP = ("z", "p", "o")


def copies_of(shards):
    return max(1, shards // (PLANE * PLANE))


def gather(x, axes):
    return lax.all_gather(x, axes, axis=0, tiled=True)


def scatter_sum(x, axes):
    return lax.psum_scatter(x.astype(jnp.bfloat16), axes, scatter_dimension=0, tiled=True)


def local(
    hidden_in,
    row_lengths,
    norm_attn,
    w_query,
    b_query,
    w_key,
    b_key,
    w_value,
    b_value,
    w_out,
    norm_mlp,
    w_gate,
    w_up,
    w_down,
    out_grad,
):
    bf = jnp.bfloat16
    quarters = lax.axis_size("z")
    lanes = lax.axis_size("head")
    lane_index = lax.axis_index("head")
    shards = quarters * PLANE
    copies = lax.axis_size("o")
    if copies > 1:
        norm_attn, norm_mlp, w_query, w_key, w_value, w_gate, w_up = [
            lax.all_gather(x, "o", axis=0, tiled=True)
            for x in (norm_attn, norm_mlp, w_query, w_key, w_value, w_gate, w_up)
        ]
        b_query, b_key, b_value, w_out, w_down = [
            lax.all_gather(x, "o", axis=1, tiled=True)
            for x in (b_query, b_key, b_value, w_out, w_down)
        ]
    local_rows = hidden_in.shape[0]
    token_count = local_rows * lanes
    depth = norm_attn.shape[0]
    width = hidden_in.shape[1]
    head_dim = w_key.shape[1]
    query_width = w_query.shape[1]
    group_heads = query_width // head_dim
    hidden_width = w_gate.shape[1]
    part_width = -(-hidden_width // (128 * quarters)) * 128
    segment, positions = layout(row_lengths[0], token_count)
    cosine, sine_tab = rotary_tables(positions, head_dim)
    cosine = cosine[:, None, :]
    sine_tab = sine_tab[:, None, :]
    place = jnp.arange(token_count, dtype=jnp.int32)
    allowed = (segment[:, None] == segment[None, :]) & (place[None, :] <= place[:, None])

    small = jnp.concatenate([norm_attn, norm_mlp, b_query[0], b_key[0], b_value[0]])
    used = small.shape[0]
    rows_used = -(-used // (128 * 16)) * 16
    small = jnp.pad(small, (0, rows_used * 128 - used)).reshape(rows_used, 128)
    attn_set, small, wg, wu, wd_rows, grad_rows = gather_all(
        jnp.concatenate([w_query, w_key, w_value, w_out.T], 1),
        small,
        w_gate,
        w_up,
        w_down.T,
        out_grad.astype(bf),
        shards,
        part_width,
    )
    attn_set = attn_set.reshape(width, attn_set.shape[2])
    small = small.reshape(shards, rows_used * 128)
    wg, wu, wd_rows = [w.reshape(width, part_width) for w in (wg, wu, wd_rows)]
    grad_rows = grad_rows.reshape(quarters, token_count, width)
    wq_full = attn_set[:, :query_width]
    wk_full = attn_set[:, query_width : query_width + head_dim]
    wv_full = attn_set[:, query_width + head_dim : query_width + 2 * head_dim]
    wo_rows = attn_set[:, query_width + 2 * head_dim :]
    cuts = [depth, depth, b_query.shape[1], b_key.shape[1], b_value.shape[1]]
    edges = [sum(cuts[:i]) for i in range(6)]
    gain_attn, gain_mlp, bias_query, bias_key, bias_value = [
        small[:, edges[i] : edges[i + 1]].reshape(-1).astype(jnp.float32) for i in range(5)
    ]

    normed_low = gather(rms_norm(hidden_in, gain_attn).astype(bf), "head")
    query_pre = product(normed_low, wq_full) + bias_query
    key_pre = product(normed_low, wk_full) + bias_key
    value_low = (product(normed_low, wv_full) + bias_value).astype(bf)
    query_rot = rotate(
        query_pre.reshape(token_count, group_heads, head_dim), cosine, sine_tab
    ).astype(bf)
    key_rot = rotate(key_pre[:, None, :], cosine, sine_tab)[:, 0].astype(bf)
    heads_out, log_sums = attend_forward(query_rot, key_rot, value_low, allowed)
    heads_low = heads_out.reshape(token_count, query_width).astype(bf)
    residual = hidden_in + scatter_sum(contract_last(heads_low, wo_rows), "head").astype(
        jnp.float32
    )
    y_half, grad_normed_mlp, *mlp_grads = mlp_all(
        rms_norm(residual, gain_mlp).astype(bf), grad_rows, wg, wu, wd_rows, hidden_width
    )
    mlp_terms = [g.reshape(shards, depth, part_width) for g in mlp_grads]

    _, mlp_pull = jax.vjp(rms_norm, residual, gain_mlp)
    grad_residual_part, grad_gain_mlp = mlp_pull(grad_normed_mlp)
    grad_residual = out_grad + grad_residual_part
    grad_attn_rows = gather(grad_residual.astype(bf), "head")
    grad_heads = product(grad_attn_rows, wo_rows).astype(bf)
    query_grad, key_grad, value_grad = attend_backward(
        query_rot,
        key_rot,
        value_low,
        allowed,
        log_sums,
        grad_heads.reshape(token_count, group_heads, head_dim),
    )
    grad_query = (
        unrotate(query_grad, cosine, sine_tab).reshape(token_count, query_width).astype(bf)
    )
    grad_key = unrotate(key_grad[:, None, :], cosine, sine_tab)[:, 0].astype(bf)
    grad_value = value_grad.astype(bf)
    grad_qkv = jnp.concatenate([grad_query, grad_key, grad_value], 1)
    grad_normed_attn = scatter_sum(
        contract_last(grad_qkv, attn_set[:, : query_width + 2 * head_dim]), "head"
    ).astype(jnp.float32)
    _, attn_pull = jax.vjp(rms_norm, hidden_in, gain_attn)
    grad_in_part, grad_gain_attn = attn_pull(grad_normed_attn)
    grad_in = grad_residual + grad_in_part
    attn_terms = jnp.concatenate(
        [contract_first(normed_low, grad_qkv), contract_first(grad_attn_rows, heads_low)], 1
    )
    bias_vec = jnp.sum(grad_qkv.astype(jnp.float32), 0)
    small_grads = jnp.concatenate([grad_gain_attn, grad_gain_mlp, bias_vec]).reshape(-1, 128)
    small_total, attn_part, y_sum, *quarter_grads = reduce_all(
        small_grads,
        attn_terms.astype(bf).reshape(shards, depth, attn_terms.shape[1]),
        *mlp_terms,
        y_half,
        shards,
    )
    def whole_rows(parts):
        taken = []
        for index in range(quarters):
            skip = max(0, index * part_width - (hidden_width - part_width))
            if skip < part_width:
                taken.append(parts[index][:, skip:])
        return jnp.concatenate(taken, 1).astype(jnp.float32)

    grad_w_gate, grad_w_up, grad_w_down = [whole_rows(parts) for parts in quarter_grads]
    if copies > 1:
        small_total = lax.psum(small_total, "o")
        attn_part, grad_w_gate, grad_w_up, grad_w_down = [
            lax.psum_scatter(x, "o", scatter_dimension=0, tiled=True)
            for x in (attn_part, grad_w_gate, grad_w_up, grad_w_down)
        ]
    grad_w_down = grad_w_down.T
    small_total = small_total.reshape(lanes, -1)
    block_out = residual + y_sum
    gain_total = jnp.sum(small_total[:, : 2 * width], 0).reshape(2, width)
    bias_total = small_total[:, 2 * width :]
    return (
        block_out,
        grad_in,
        gain_total[0],
        attn_part[:, :query_width],
        bias_total[:, :query_width],
        attn_part[:, query_width : query_width + head_dim],
        bias_total[:, query_width : query_width + head_dim],
        attn_part[:, query_width + head_dim : query_width + 2 * head_dim],
        bias_total[:, query_width + head_dim :],
        attn_part[:, query_width + 2 * head_dim :].T,
        gain_total[1],
        grad_w_gate,
        grad_w_up,
        grad_w_down,
    )


def solution(mesh):
    shards = mesh.shape["dp"]
    shape = (shards // (PLANE * copies_of(shards)), PLANE, copies_of(shards), mesh.shape["head"])
    split = jax.sharding.Mesh(mesh.devices.reshape(shape), DP + ("head",))
    rows = P(DP + ("head",), None)
    deep = P(DP, "head")
    wide = P("head", DP)
    placed = (
        rows, P(DP, None), P(DP), deep, wide, deep, wide, deep, wide, wide, P(DP), deep, deep, wide, rows
    )
    return jax.shard_map(
        local,
        mesh=split,
        in_specs=placed,
        out_specs=(
            rows,
            rows,
            P(),
            deep,
            P(),
            deep,
            P(),
            deep,
            P(),
            wide,
            P(),
            deep,
            deep,
            wide,
        ),
        check_vma=False,
    )
```

```python
import functools
import math

import jax
import jax.numpy as jnp
from jax import lax
from jax.experimental import pallas as pl
from jax.experimental.pallas import tpu as pltpu
from jax.sharding import PartitionSpec as P

NORM_EPS = 1e-06
ROPE_BASE = 1000000.0
MASKED = -1e30
MESH_ID = pl.DeviceIdType.MESH
PLANE = 4
DP = ("z", "p", "o")
LANE = 128
TILE = 256
BF = jnp.bfloat16
F32 = jnp.float32


def layout(lengths_row, token_count):
    row_ends = jnp.cumsum(lengths_row)
    places = jnp.arange(token_count, dtype=jnp.int32)
    passed = (places[:, None] >= row_ends[None, :]).astype(jnp.int32)
    segment = jnp.sum(passed, axis=1)
    offset = jnp.sum(passed * lengths_row[None, :], axis=1)
    return (segment, places - offset)


def rotary_tables(positions, head_dim):
    half_dim = head_dim // 2
    frequency = jnp.exp(
        jnp.arange(half_dim, dtype=F32) * (-2.0 * math.log(ROPE_BASE) / head_dim)
    )
    angles = positions.astype(F32)[:, None] * frequency[None, :]
    cosine = jnp.cos(angles)
    sine_tab = jnp.sin(angles)
    return (jnp.concatenate([cosine, cosine], -1), jnp.concatenate([-sine_tab, sine_tab], -1))


def dot(left, right):
    return jnp.dot(left, right, preferred_element_type=F32)


def dot_last(left, right):
    return lax.dot_general(left, right, (((1,), (1,)), ((), ())), preferred_element_type=F32)


def dot_first(left, right):
    return lax.dot_general(left, right, (((0,), (0,)), ((), ())), preferred_element_type=F32)


def flipped(index, mask):
    bit = 1
    while bit <= mask:
        if mask & bit:
            index = index + bit - 2 * bit * lax.rem(lax.div(index, bit), 2)
        bit *= 2
    return index


def moved(index, other, count):
    total, bit = 0, 1
    while bit < count:
        a, b = lax.rem(lax.div(index, bit), 2), lax.rem(lax.div(other, bit), 2)
        total = total + bit * (a + b - 2 * a * b)
        bit *= 2
    return total


def spot(z, p, c):
    return {"z": z, "p": p, "head": c}


def here():
    return (lax.axis_index("z"), lax.axis_index("p"), lax.axis_index("head"))


def greet(peers):
    bar = pltpu.get_barrier_semaphore()
    for peer in peers:
        pl.semaphore_signal(bar, inc=1, device_id=peer, device_id_type=MESH_ID)
    pl.semaphore_wait(bar, len(peers))


def push(src, dst, ssem, rsem, peer):
    copy = pltpu.make_async_remote_copy(
        src_ref=src, dst_ref=dst, send_sem=ssem, recv_sem=rsem,
        device_id=peer, device_id_type=MESH_ID,
    )
    copy.start()
    return copy


def landed(ref, sem):
    pltpu.make_async_copy(ref, ref, sem).wait()


def line_of(table, start, count):
    return jnp.concatenate([table[i : i + 1, :] for i in range(start, start + count)], axis=1)


def wide_mean(value):
    return jnp.mean(value, axis=-1, keepdims=True)


def softmax_of(query, key, mask_bias):
    scores = dot_last(query, key) * (1.0 / math.sqrt(query.shape[-1])) + mask_bias
    top = jnp.max(scores, axis=-1, keepdims=True)
    exp_scores = jnp.exp(scores - top)
    return exp_scores / jnp.sum(exp_scores, axis=-1, keepdims=True)


def gather_kernel(
    quarters,
    part_cols,
    aset,
    vec,
    gate,
    up,
    down,
    grad,
    hidden,
    cosine,
    sine_tab,
    mask_bias,
    aset_all,
    vec_sum,
    gate_all,
    up_all,
    down_all,
    grad_all,
    h1_all,
    q_out,
    k_out,
    v_out,
    o_out,
    r1_out,
    h2_out,
    vec_all,
    halves,
    pair_out,
    pair_in,
    a_send,
    a_recv,
    m_send,
    m_recv,
    s_send,
    s_recv,
    g_send,
    g_recv,
    p_send,
    p_recv,
    l_sem,
):
    z, p, c = here()
    dp = z * PLANE + p
    units = gate.shape[1]
    shards, depth = aset_all.shape[:2]
    rows, width = hidden.shape
    head_dim = cosine.shape[1]
    query_width = q_out.shape[1]
    qkv_width = query_width + 2 * head_dim
    group_heads = query_width // head_dim
    wide = width // LANE

    def at(zz, pp):
        return spot(zz, pp, c)

    pair = spot(z, p, 1 - c)
    masks = [(kz, kp) for kz in range(quarters) for kp in range(PLANE) if kz or kp]
    greet([at(flipped(z, kz), flipped(p, kp)) for kz, kp in masks] + [pair])

    px, py = flipped(p, 1), flipped(p, 2)
    sent = []

    def send(*args):
        sent.append(push(*args))

    def cols_of(weight, quarter):
        first = jnp.minimum(quarter * part_cols, units - part_cols)
        return weight.at[:, pl.ds(pl.multiple_of(first, LANE), part_cols)]

    sets = [(aset_all, lambda zz: aset, a_send, a_recv)] + [
        (whole, functools.partial(cols_of, weight), m_send.at[i], m_recv.at[i])
        for i, (whole, weight) in enumerate(((gate_all, gate), (up_all, up), (down_all, down)))
    ]

    def line(s, k):
        whole, part, ss, rs = sets[s]
        zz = flipped(z, k)
        send(part(zz), whole.at[dp], ss.at[k, 0], rs.at[k, 0], at(zz, p))

    def came(s, k, role):
        whole, _, _, rs = sets[s]
        landed(whole.at[flipped(z, k) * PLANE + flipped(p, role)], rs.at[k, role])

    def fan(s, k):
        whole, part, ss, rs = sets[s]
        slot = flipped(z, k) * PLANE + p
        src = whole.at[slot] if k else part(z)
        if k:
            came(s, k, 0)
        send(src, whole.at[slot], ss.at[k, 1], rs.at[k, 1], at(z, px))
        send(src, whole.at[slot], ss.at[k, 2], rs.at[k, 2], at(z, py))

    def relay(s, k):
        whole, _, ss, rs = sets[s]
        role = 1 if k % 2 == 0 else 2
        came(s, k, role)
        slot = flipped(z, k) * PLANE + flipped(p, role)
        to = py if role == 1 else px
        send(whole.at[slot], whole.at[slot], ss.at[k, 3], rs.at[k, 3], at(z, to))

    def rest(s, k):
        came(s, k, 2 if k % 2 == 0 else 1)
        came(s, k, 3)

    others = range(1, quarters)
    for n, (kz, kp) in enumerate(masks):
        send(vec, vec_all.at[dp], s_send.at[n], s_recv.at[n], at(flipped(z, kz), flipped(p, kp)))
    local = [
        pltpu.make_async_copy(vec, vec_all.at[dp], l_sem.at[0]),
        pltpu.make_async_copy(aset, aset_all.at[dp], l_sem.at[1]),
        pltpu.make_async_copy(cols_of(gate, z), gate_all.at[dp], l_sem.at[2]),
        pltpu.make_async_copy(cols_of(up, z), up_all.at[dp], l_sem.at[3]),
        pltpu.make_async_copy(cols_of(down, z), down_all.at[dp], l_sem.at[4]),
        pltpu.make_async_copy(grad, grad_all.at[0, c], l_sem.at[5]),
    ]
    fan(0, 0)
    for k in others:
        line(0, k)
    for s in (1, 2, 3):
        for k in others:
            line(s, k)
    for copy in local:
        copy.start()
    send(grad, grad_all.at[0, c], g_send.at[0, 1], g_recv.at[0, 1], pair)
    for k in others:
        send(grad, grad_all.at[k, c], g_send.at[k, 0], g_recv.at[k, 0], at(flipped(z, k), p))
    fan(1, 0)

    local[0].wait()
    for n, (kz, kp) in enumerate(masks):
        landed(vec_all.at[flipped(z, kz) * PLANE + flipped(p, kp)], s_recv.at[n])
    total = vec_all[0].astype(F32)
    for i in range(1, shards):
        total = total + vec_all[i].astype(F32)
    vec_sum[...] = total
    x = hidden[...]
    normed = x * lax.rsqrt(wide_mean(x * x) + NORM_EPS) * line_of(total, 0, wide)
    h1_all[c] = normed.astype(BF)
    send(h1_all.at[c], h1_all.at[c], p_send.at[0], p_recv.at[0], pair)

    relay(0, 0)
    for k in others:
        fan(0, k)
    fan(2, 0)
    fan(3, 0)
    for k in others:
        relay(0, k)
    relay(1, 0)
    local[1].wait()
    for k in range(quarters):
        rest(0, k)
    landed(h1_all.at[1 - c], p_recv.at[0])

    def project(n):
        cols = slice(n * TILE, (n + 1) * TILE)
        weight = aset_all[:, :, cols].reshape(width, TILE)
        out = dot(h1_all[...].reshape(2 * rows, width), weight)
        out = out + line_of(vec_sum[...], 2 * wide + n * TILE // LANE, TILE // LANE)
        for j in range(TILE // head_dim):
            head = n * TILE // head_dim + j
            u = out[:, j * head_dim : (j + 1) * head_dim]
            if head <= group_heads:
                u = u * cosine[...] + pltpu.roll(u, head_dim // 2, 1) * sine_tab[...]
            u = u.astype(BF)
            if head < group_heads:
                q_out[:, head * head_dim : (head + 1) * head_dim] = u
            elif head == group_heads:
                k_out[...] = u
            else:
                v_out[...] = u

    def attend(head):
        cols = slice(head * head_dim, (head + 1) * head_dim)
        probs = softmax_of(q_out[:, cols], k_out[...], mask_bias[...])
        o_out[:, cols] = dot(probs.astype(BF), v_out[...]).astype(BF)

    def leave(i):
        half = shards // 2
        weight = aset_all[i * half : (i + 1) * half, :, qkv_width:].reshape(width // 2, query_width)
        out = dot_last(o_out[...], weight)
        cols = slice(i * width // 2, (i + 1) * width // 2)
        halves[0, :, cols] = out[:rows]
        halves[1, :, cols] = out[rows:]

    def swap():
        pair_out[...] = halves[1 - c].astype(BF)
        send(pair_out, pair_in, p_send.at[1], p_recv.at[1], pair)

    def enter():
        landed(pair_in, p_recv.at[1])
        residual = hidden[...] + halves[c] + pair_in[...].astype(F32)
        r1_out[...] = residual
        gain = line_of(vec_sum[...], wide, wide)
        h2_out[...] = (residual * lax.rsqrt(wide_mean(residual * residual) + NORM_EPS) * gain).astype(BF)

    work = [functools.partial(project, n) for n in range(qkv_width // TILE)]
    work += [functools.partial(attend, head) for head in range(group_heads)]
    work += [functools.partial(leave, i) for i in range(2)] + [swap, enter]
    moves = [functools.partial(fan, 1, k) for k in others]
    moves += [functools.partial(relay, s, 0) for s in (2, 3)]
    for k in others:
        moves += [functools.partial(fan, 2, k), functools.partial(relay, 1, k)]
    for k in others:
        moves += [functools.partial(fan, 3, k), functools.partial(relay, 2, k)]
    moves += [functools.partial(relay, 3, k) for k in others]
    for i in range(max(len(work), len(moves))):
        if i < len(moves):
            moves[i]()
        if i < len(work):
            work[i]()
    for k in others:
        slot = grad_all.at[k, c]
        landed(slot, g_recv.at[k, 0])
        send(slot, slot, g_send.at[k, 1], g_recv.at[k, 1], pair)
    for k in range(quarters):
        landed(grad_all.at[k, 1 - c], g_recv.at[k, 1])
    for s in (1, 2, 3):
        for k in range(quarters):
            rest(s, k)
    for copy in local[2:]:
        copy.wait()
    for copy in sent:
        copy.wait_send()


def gather_all(aset, vec, gate, up, down, grad, hidden, cosine, sine_tab, mask_bias, quarters, part_cols):
    shards = quarters * PLANE
    depth, query_width = aset.shape[0], aset.shape[1]
    head_dim = cosine.shape[1]
    query_width = (aset.shape[1] - 2 * head_dim) // 2
    rows, width = hidden.shape
    dma = pltpu.SemaphoreType.DMA
    hbm = pl.BlockSpec(memory_space=pl.ANY)
    vmem = pl.BlockSpec(memory_space=pltpu.VMEM)
    shape = jax.ShapeDtypeStruct
    part = shape((shards, depth, part_cols), BF)
    return pl.pallas_call(
        functools.partial(gather_kernel, quarters, part_cols),
        out_shape=(
            shape((shards,) + aset.shape, BF),
            shape(vec.shape, F32),
            part,
            part,
            part,
            shape((quarters, 2) + grad.shape, BF),
            shape((2, rows, width), BF),
            shape((2 * rows, query_width), BF),
            shape((2 * rows, head_dim), BF),
            shape((2 * rows, head_dim), BF),
            shape((2 * rows, query_width), BF),
            shape((rows, width), F32),
            shape((rows, width), BF),
        ),
        in_specs=[hbm] * 6 + [vmem] * 4,
        out_specs=[vmem] * 2 + [hbm] * 4 + [vmem] * 7,
        scratch_shapes=[
            pltpu.VMEM((shards,) + vec.shape, BF),
            pltpu.VMEM((2, rows, width), F32),
            pltpu.VMEM((rows, width), BF),
            pltpu.VMEM((rows, width), BF),
            dma((quarters, 4)),
            dma((quarters, 4)),
            dma((3, quarters, 4)),
            dma((3, quarters, 4)),
            dma((shards - 1,)),
            dma((shards - 1,)),
            dma((quarters, 2)),
            dma((quarters, 2)),
            dma((2,)),
            dma((2,)),
            dma((6,)),
        ],
        compiler_params=pltpu.CompilerParams(
            collective_id=0, has_side_effects=True, vmem_limit_bytes=40 * 2**20
        ),
    )(aset, vec, gate, up, down, grad, hidden, cosine, sine_tab, mask_bias)


def mlp_kernel(
    quarters,
    hidden,
    own,
    grads,
    gate,
    up,
    down,
    y_out,
    d_out,
    gate_out,
    up_out,
    down_out,
    h_all,
    g_all,
    w_all,
    act,
    d_gate,
    d_up,
    y_part,
    d_part,
    y_slot,
    d_slot,
    d_line,
    h_send,
    h_recv,
    hp_send,
    hp_recv,
    y_send,
    y_recv,
    d_send,
    d_recv,
    l_send,
    l_recv,
    load_sem,
    out_sem,
):
    z, p, c = here()
    pair = spot(z, p, 1 - c)
    rows, width = own.shape
    part_cols = gate.shape[1]
    padded = w_all.shape[2]
    tiles = padded // TILE

    def half(k, lane):
        return h_all.at[k, pl.ds(pl.multiple_of(lane * rows, 16), rows)]

    loads = [
        pltpu.make_async_copy(w, w_all.at[i, :, pl.ds(0, part_cols)], load_sem.at[i])
        for i, w in enumerate((gate, up, down))
    ] + [pltpu.make_async_copy(grads, g_all, load_sem.at[3]), pltpu.make_async_copy(own, half(0, c), load_sem.at[4])]
    for copy in loads:
        copy.start()
    greet([spot(flipped(z, k), p, c) for k in range(1, quarters)] + [pair])
    push(own, half(0, c), hp_send.at[0], hp_recv.at[0], pair)
    for k in range(1, quarters):
        push(own, half(k, c), h_send.at[k], h_recv.at[k], spot(flipped(z, k), p, c))
    if padded > part_cols:
        for i in range(3):
            w_all[i, :, part_cols:] = jnp.zeros((width, padded - part_cols), w_all.dtype)
    first = jnp.minimum(z * part_cols, hidden - part_cols)
    skip = z * part_cols - first
    for copy in loads:
        copy.wait()

    def finish(k):
        mine, other = (y_part.at[k, c], y_slot.at[k])
        landed(other, y_recv.at[k])
        other[...] = (other[...].astype(F32) + mine[...].astype(F32)).astype(other.dtype)
        pltpu.make_async_copy(other, y_out.at[k], out_sem.at[0, k]).start()
        mine, other = (d_part.at[k, c], d_slot.at[k])
        landed(other, d_recv.at[k])
        other[...] = (other[...].astype(F32) + mine[...].astype(F32)).astype(other.dtype)

        @pl.when(k > 0)
        def _():
            push(other, d_line.at[k], l_send.at[k], l_recv.at[k], spot(moved(z, k, quarters), p, c))

    def block(k, carry):
        @pl.when(k > 0)
        def _():
            landed(half(k, c), h_recv.at[k])
            push(half(k, c), half(k, c), hp_send.at[k], hp_recv.at[k], pair)

        landed(half(k, 1 - c), hp_recv.at[k])

        def units(n, carry):
            cols = pl.ds(pl.multiple_of(n * TILE, TILE), TILE)
            h = h_all[k]
            g = jnp.dot(h, w_all[0, :, cols], preferred_element_type=F32)
            u = jnp.dot(h, w_all[1, :, cols], preferred_element_type=F32)
            da = jnp.dot(g_all[k], w_all[2, :, cols], preferred_element_type=F32)
            column = n * TILE + lax.broadcasted_iota(jnp.int32, (1, TILE), 1)
            ok = column >= skip
            g = jnp.where(ok, g, 0.0)
            u = jnp.where(ok, u, 0.0)
            s = 1.0 / (1.0 + jnp.exp(-g))
            sg = g * s
            act[k, :, cols] = (sg * u).astype(BF)
            d_gate[k, :, cols] = (da * u * s * (1.0 + g * (1.0 - s))).astype(BF)
            d_up[k, :, cols] = (da * sg).astype(BF)
            return carry

        lax.fori_loop(0, tiles, units, 0)

        @pl.when(k > 0)
        def _():
            finish(k - 1)

        def model(n, carry):
            cols = pl.ds(pl.multiple_of(n * TILE, TILE), TILE)

            def back(left, index):
                return lax.dot_general(
                    left[k], w_all[index, cols, :], (((1,), (1,)), ((), ())),
                    preferred_element_type=F32,
                )

            y = back(act, 2).astype(BF)
            d = (back(d_gate, 0) + back(d_up, 1)).astype(BF)
            for lane in range(2):
                y_part[k, lane, :, cols] = y[lane * rows : (lane + 1) * rows]
                d_part[k, lane, :, cols] = d[lane * rows : (lane + 1) * rows]
            return carry

        lax.fori_loop(0, width // TILE, model, 0)
        push(y_part.at[k, 1 - c], y_slot.at[k], y_send.at[k], y_recv.at[k], pair)
        push(d_part.at[k, 1 - c], d_slot.at[k], d_send.at[k], d_recv.at[k], pair)
        return carry

    lax.fori_loop(0, quarters, block, 0)
    finish(quarters - 1)

    outs = (gate_out, up_out, down_out)

    def weight(n, carry):
        cols = pl.ds(pl.multiple_of(n * TILE, TILE), TILE)
        for i, (left, right) in enumerate(((h_all, d_gate), (h_all, d_up), (g_all, act))):
            total = None
            for k in range(quarters):
                term = lax.dot_general(
                    left[k, :, cols], right[k], (((0,), (0,)), ((), ())),
                    preferred_element_type=F32,
                )
                total = term if total is None else total + term
            w_all[i, cols, :] = total.astype(BF)
            pltpu.make_async_copy(
                w_all.at[i, cols, pl.ds(0, part_cols)], outs[i].at[cols, :], out_sem.at[1 + i, n]
            ).start()
        return carry

    lax.fori_loop(0, width // TILE, weight, 0)
    total = d_slot[0].astype(F32)
    for k in range(1, quarters):
        landed(d_line.at[k], l_recv.at[k])
        total = total + d_line[k].astype(F32)
    d_out[...] = total
    for n in range(width // TILE):
        for i in range(3):
            tile = w_all.at[i, pl.ds(n * TILE, TILE), pl.ds(0, part_cols)]
            pltpu.make_async_copy(tile, outs[i].at[pl.ds(n * TILE, TILE), :], out_sem.at[1 + i, n]).wait()
    for k in range(quarters):
        pltpu.make_async_copy(y_slot.at[k], y_out.at[k], out_sem.at[0, k]).wait()
        landed(half(k, c), hp_send.at[k])
        landed(y_part.at[k, 1 - c], y_send.at[k])
        landed(d_part.at[k, 1 - c], d_send.at[k])
        if k:
            landed(own, h_send.at[k])
            landed(d_slot.at[k], l_send.at[k])


def mlp_all(own, grads, gate, up, down, hidden):
    bf = jnp.bfloat16
    quarters, block_rows, width = grads.shape
    part_cols = gate.shape[1]
    padded = -(-part_cols // TILE) * TILE
    rows = own.shape[0]
    dma = pltpu.SemaphoreType.DMA
    hbm = pl.BlockSpec(memory_space=pl.ANY)
    vmem = pl.BlockSpec(memory_space=pltpu.VMEM)
    grad_w = jax.ShapeDtypeStruct((width, part_cols), bf)
    steps = max(quarters, width // TILE)
    return pl.pallas_call(
        functools.partial(mlp_kernel, quarters, hidden),
        out_shape=(
            jax.ShapeDtypeStruct((quarters, rows, width), bf),
            jax.ShapeDtypeStruct((rows, width), F32),
            grad_w,
            grad_w,
            grad_w,
        ),
        in_specs=[hbm] * 5,
        out_specs=[hbm, vmem, hbm, hbm, hbm],
        scratch_shapes=[
            pltpu.VMEM((quarters, block_rows, width), bf),
            pltpu.VMEM((quarters, block_rows, width), bf),
            pltpu.VMEM((3, width, padded), bf),
            pltpu.VMEM((quarters, block_rows, padded), bf),
            pltpu.VMEM((quarters, block_rows, padded), bf),
            pltpu.VMEM((quarters, block_rows, padded), bf),
            pltpu.VMEM((quarters, 2, rows, width), bf),
            pltpu.VMEM((quarters, 2, rows, width), bf),
            pltpu.VMEM((quarters, rows, width), bf),
            pltpu.VMEM((quarters, rows, width), bf),
            pltpu.VMEM((quarters, rows, width), bf),
        ]
        + [dma((quarters,))] * 10
        + [dma((5,)), dma((4, steps))],
        compiler_params=pltpu.CompilerParams(
            collective_id=2, has_side_effects=True, vmem_limit_bytes=60 * 2**20
        ),
    )(own, grads, gate, up, down)


AHEAD = 1
LAG = 1


def reduce_kernel(
    quarters,
    gate,
    up,
    down,
    y_half,
    d_sum,
    r1,
    out_grad,
    hidden,
    h1_all,
    q_in,
    k_in,
    v_in,
    o_in,
    aset_all,
    vec_sum,
    cosine,
    sine_tab,
    mask_bias,
    small_sum,
    attn_sum,
    block_out,
    grad_in,
    gate_out,
    up_out,
    down_out,
    small,
    small_all,
    staged,
    attn_slots,
    mlp_slots,
    mlp_own,
    attn_line,
    y_line,
    attn_grads,
    da_all,
    dr1,
    do_all,
    dqkv,
    dk_sum,
    dv_sum,
    halves,
    pair_out,
    pair_in,
    t_send,
    t_recv,
    z_send,
    z_recv,
    s_send,
    s_recv,
    y_send,
    y_recv,
    p_send,
    p_recv,
    l_sem,
    own_sem,
):
    z, p, c = here()
    dp = z * PLANE + p
    pair = spot(z, p, 1 - c)
    shards, depth, attn_width = aset_all.shape
    rows, width = r1.shape
    head_dim = cosine.shape[1]
    query_width = q_in.shape[1]
    qkv_width = query_width + 2 * head_dim
    group_heads = query_width // head_dim
    wide = width // LANE
    others = range(1, quarters)
    scale = 1.0 / math.sqrt(head_dim)
    sources = (attn_grads, gate, up, down)
    outs = (None, gate_out, up_out, down_out)

    def source(s, k, kp):
        return sources[s].at[flipped(z, k) * PLANE + flipped(p, kp)]

    ks = list(others) + [0]
    units = [(s, k) for i in range(0, quarters, 2) for s in (1, 2, 3) for k in ks[i : i + 2]]
    for s, k in units:
        for i, kp in enumerate((0, 2 - k % 2)):
            pltpu.make_async_copy(source(s, k, kp), mlp_own.at[s - 1, k, i], own_sem.at[s - 1, k, i]).start()
    first_y = pltpu.make_async_copy(y_half.at[0], y_line.at[0], l_sem.at[0])
    first_y.start()
    masks = [(kz, kp) for kz in range(quarters) for kp in range(PLANE) if kz or kp]
    greet([spot(flipped(z, kz), flipped(p, kp), c) for kz, kp in masks] + [pair])
    sent = []
    local = []

    def send(*args):
        sent.append(push(*args))

    side = [spot(z, flipped(p, 1), c), spot(z, flipped(p, 2), c)]

    def slots(s, k, role):
        return attn_slots.at[k, role] if s == 0 else mlp_slots.at[s - 1, k, role]

    def term(s, k, i):
        if s == 0:
            return source(s, k, (0, 2 - k % 2)[i])
        return mlp_own.at[s - 1, k, i]

    def ready(s, k, i):
        if s:
            landed(mlp_own.at[s - 1, k, i], own_sem.at[s - 1, k, i])

    def first(s, k):
        way = k % 2
        send(source(s, k, 3), slots(s, k, 0), t_send.at[s, k, 0], t_recv.at[s, k, 0], side[way])
        send(source(s, k, 1 + way), slots(s, k, 1), t_send.at[s, k, 1], t_recv.at[s, k, 1], side[way])

    def relay(s, k):
        slot = slots(s, k, 0)
        ready(s, k, 1)
        landed(slot, t_recv.at[s, k, 0])
        slot[...] = (slot[...].astype(F32) + term(s, k, 1)[...].astype(F32)).astype(BF)
        send(slot, slots(s, k, 2), t_send.at[s, k, 2], t_recv.at[s, k, 2], side[1 - k % 2])

    def last(s, k):
        one, two = (slots(s, k, 1), slots(s, k, 2))
        ready(s, k, 0)
        landed(one, t_recv.at[s, k, 1])
        landed(two, t_recv.at[s, k, 2])
        total = term(s, k, 0)[...].astype(F32) + one[...].astype(F32) + two[...].astype(F32)
        one[...] = total.astype(BF)
        if s == 0:
            if k:
                send(one, attn_line.at[k], z_send.at[s, k], z_recv.at[s, k], spot(flipped(z, k), p, c))
        elif k:
            send(one, outs[s].at[z], z_send.at[s, k], z_recv.at[s, k], spot(flipped(z, k), p, c))
        else:
            copy = pltpu.make_async_copy(one, outs[s].at[z], l_sem.at[s])
            copy.start()
            local.append(copy)

    def note(value, start):
        for i in range(value.shape[1] // LANE):
            small[start + i : start + i + 1, :] = value[:, i * LANE : (i + 1) * LANE]

    def norm_back():
        residual, dh2 = (r1[...], d_sum[...])
        rho = lax.rsqrt(wide_mean(residual * residual) + NORM_EPS)
        n = residual * rho
        inner = dh2 * line_of(vec_sum[...], wide, wide)
        note(jnp.sum(dh2 * n, axis=0, keepdims=True), wide)
        total = out_grad[...] + rho * (inner - n * wide_mean(inner * n))
        dr1[...] = total
        da_all[c] = total.astype(BF)
        send(da_all.at[c], da_all.at[c], p_send.at[0], p_recv.at[0], pair)

    def heads_back(n):
        if n == 0:
            landed(da_all.at[1 - c], p_recv.at[0])
        cols = slice(n * TILE, (n + 1) * TILE)
        weight = aset_all[:, :, qkv_width + n * TILE : qkv_width + (n + 1) * TILE]
        do_all[:, cols] = dot(da_all[...].reshape(2 * rows, width), weight.reshape(width, TILE)).astype(BF)

    def unrotate(value):
        return value * cosine[...] - pltpu.roll(value, head_dim // 2, 1) * sine_tab[...]

    def attend_back(head):
        cols = slice(head * head_dim, (head + 1) * head_dim)
        query, grad = (q_in[:, cols], do_all[:, cols])
        probs = softmax_of(query, k_in[...], mask_bias[...])
        grad_probs = dot_last(grad, v_in[...])
        centre = jnp.sum(grad_probs * probs, axis=-1, keepdims=True)
        grad_scores = (probs * (grad_probs - centre) * scale).astype(BF)
        dqkv[:, cols] = unrotate(dot(grad_scores, k_in[...])).astype(BF)
        key_term = dot_first(grad_scores, query)
        value_term = dot_first(probs.astype(BF), grad)
        dk_sum[...] = key_term if head == 0 else dk_sum[...] + key_term
        dv_sum[...] = value_term if head == 0 else dv_sum[...] + value_term

    def keys_back():
        dqkv[:, query_width : query_width + head_dim] = unrotate(dk_sum[...]).astype(BF)
        dqkv[:, query_width + head_dim :] = dv_sum[...].astype(BF)
        note(jnp.sum(dqkv[...].astype(F32), axis=0, keepdims=True), 2 * wide)

    def inputs_back(i):
        half = shards // 2
        weight = aset_all[i * half : (i + 1) * half, :, :qkv_width].reshape(width // 2, qkv_width)
        out = dot_last(dqkv[...], weight)
        cols = slice(i * width // 2, (i + 1) * width // 2)
        halves[0, :, cols] = out[:rows]
        halves[1, :, cols] = out[rows:]
        if i:
            pair_out[...] = halves[1 - c].astype(BF)
            send(pair_out, pair_in, p_send.at[1], p_recv.at[1], pair)

    def weights_back(i):
        cols = slice(i * 4 * depth, (i + 1) * 4 * depth)
        blocks = slice(i * 4, (i + 1) * 4)
        left = h1_all[:, :, cols].reshape(2 * rows, 4 * depth)
        attn_grads[blocks, :, :qkv_width] = (
            dot_first(left, dqkv[...]).astype(BF).reshape(4, depth, qkv_width)
        )
        left = da_all[:, :, cols].reshape(2 * rows, 4 * depth)
        attn_grads[blocks, :, qkv_width:] = (
            dot_first(left, o_in[...]).astype(BF).reshape(4, depth, query_width)
        )

    def leave():
        landed(pair_in, p_recv.at[1])
        x = hidden[...]
        dh1 = halves[c] + pair_in[...].astype(F32)
        rho = lax.rsqrt(wide_mean(x * x) + NORM_EPS)
        n = x * rho
        inner = dh1 * line_of(vec_sum[...], 0, wide)
        note(jnp.sum(dh1 * n, axis=0, keepdims=True), 0)
        grad_in[...] = dr1[...] + rho * (inner - n * wide_mean(inner * n))
        for n, (kz, kp) in enumerate(masks):
            peer = spot(flipped(z, kz), flipped(p, kp), c)
            send(small, small_all.at[dp], s_send.at[n], s_recv.at[n], peer)
        small_all[dp] = small[...]

    work = [norm_back] + [functools.partial(heads_back, n) for n in range(query_width // TILE)]
    work += [functools.partial(attend_back, head) for head in range(group_heads)]
    work += [keys_back] + [functools.partial(inputs_back, i) for i in range(2)]
    work += [functools.partial(weights_back, i) for i in range(shards // 4)] + [leave]

    mlp_count = len(units)
    for k in others:
        send(y_half.at[k], y_line.at[k], y_send.at[k], y_recv.at[k], spot(flipped(z, k), p, c))
    units += [(0, k) for k in ks]
    for i in range(-AHEAD, len(units) + LAG):
        if i + AHEAD == mlp_count:
            while work:
                work.pop(0)()
        if 0 <= i + AHEAD < len(units):
            first(*units[i + AHEAD])
        if 0 <= i < len(units):
            relay(*units[i])
        if 0 <= i - LAG:
            last(*units[i - LAG])
        for _ in range(2):
            if work:
                work.pop(0)()
    for n, (kz, kp) in enumerate(masks):
        landed(small_all.at[flipped(z, kz) * PLANE + flipped(p, kp)], s_recv.at[n])
    total = small_all[0]
    for i in range(1, shards):
        total = total + small_all[i]
    staged[...] = total
    small_sum[c] = total
    send(staged, small_sum.at[c], s_send.at[len(masks)], s_recv.at[len(masks)], pair)
    first_y.wait()
    total = r1[...] + y_line[0].astype(F32)
    for k in others:
        landed(y_line.at[k], y_recv.at[k])
        total = total + y_line[k].astype(F32)
    block_out[...] = total
    landed(small_sum.at[1 - c], s_recv.at[len(masks)])
    total = attn_slots[0, 1].astype(F32)
    for k in others:
        landed(attn_line.at[k], z_recv.at[0, k])
        total = total + attn_line[k].astype(F32)
    attn_sum[...] = total
    for s in (1, 2, 3):
        for k in others:
            landed(outs[s].at[flipped(z, k)], z_recv.at[s, k])
    for copy in local:
        copy.wait()
    for copy in sent:
        copy.wait_send()


def reduce_all(quarters, mlp_grads, y_half, d_sum, r1, out_grad, hidden, h1_all, heads, aset_all, vec_sum, tables):
    shards = quarters * PLANE
    dma = pltpu.SemaphoreType.DMA
    depth, part_cols = mlp_grads[0].shape[1:]
    rows, width = r1.shape
    tokens, query_width = heads[0].shape
    head_dim = heads[1].shape[1]
    qkv_width = query_width + 2 * head_dim
    attn_shape = aset_all.shape[1:]
    vec_shape = vec_sum.shape
    vmem = pl.BlockSpec(memory_space=pltpu.VMEM)
    hbm = pl.BlockSpec(memory_space=pl.ANY)
    shape = jax.ShapeDtypeStruct
    quarter_out = shape((quarters, depth, part_cols), BF)
    return pl.pallas_call(
        functools.partial(reduce_kernel, quarters),
        out_shape=(
            shape((2,) + vec_shape, F32),
            shape(attn_shape, F32),
            shape((rows, width), F32),
            shape((rows, width), F32),
            quarter_out,
            quarter_out,
            quarter_out,
        ),
        in_specs=[hbm] * 4 + [vmem] * 14,
        out_specs=[vmem] * 4 + [hbm] * 3,
        scratch_shapes=[
            pltpu.VMEM(vec_shape, F32),
            pltpu.VMEM((shards,) + vec_shape, F32),
            pltpu.VMEM(vec_shape, F32),
            pltpu.VMEM((quarters, 3) + attn_shape, BF),
            pltpu.VMEM((3, quarters, 3, depth, part_cols), BF),
            pltpu.VMEM((3, quarters, 2, depth, part_cols), BF),
            pltpu.VMEM((quarters,) + attn_shape, BF),
            pltpu.VMEM((quarters, rows, width), BF),
            pltpu.VMEM((shards,) + attn_shape, BF),
            pltpu.VMEM((2, rows, width), BF),
            pltpu.VMEM((rows, width), F32),
            pltpu.VMEM((tokens, query_width), BF),
            pltpu.VMEM((tokens, qkv_width), BF),
            pltpu.VMEM((tokens, head_dim), F32),
            pltpu.VMEM((tokens, head_dim), F32),
            pltpu.VMEM((2, rows, width), F32),
            pltpu.VMEM((rows, width), BF),
            pltpu.VMEM((rows, width), BF),
            dma((4, quarters, 3)),
            dma((4, quarters, 3)),
            dma((4, quarters)),
            dma((4, quarters)),
            dma((shards,)),
            dma((shards,)),
            dma((quarters,)),
            dma((quarters,)),
            dma((2,)),
            dma((2,)),
            dma((4,)),
            dma((3, quarters, 2)),
        ],
        compiler_params=pltpu.CompilerParams(
            collective_id=1, has_side_effects=True, vmem_limit_bytes=60 * 2**20
        ),
    )(*mlp_grads, y_half, d_sum, r1, out_grad, hidden, h1_all, *heads, aset_all, vec_sum, *tables)


def local(
    hidden_in,
    row_lengths,
    norm_attn,
    w_query,
    b_query,
    w_key,
    b_key,
    w_value,
    b_value,
    w_out,
    norm_mlp,
    w_gate,
    w_up,
    w_down,
    out_grad,
):
    quarters = lax.axis_size("z")
    lanes = lax.axis_size("head")
    shards = quarters * PLANE
    copies = lax.axis_size("o")
    if copies > 1:
        norm_attn, norm_mlp, w_query, w_key, w_value, w_gate, w_up = [
            lax.all_gather(x, "o", axis=0, tiled=True)
            for x in (norm_attn, norm_mlp, w_query, w_key, w_value, w_gate, w_up)
        ]
        b_query, b_key, b_value, w_out, w_down = [
            lax.all_gather(x, "o", axis=1, tiled=True)
            for x in (b_query, b_key, b_value, w_out, w_down)
        ]
    token_count = hidden_in.shape[0] * lanes
    depth = norm_attn.shape[0]
    width = hidden_in.shape[1]
    head_dim = w_key.shape[1]
    query_width = w_query.shape[1]
    hidden_width = w_gate.shape[1]
    part_width = -(-hidden_width // (LANE * quarters)) * LANE
    segment, positions = layout(row_lengths[0], token_count)
    place = jnp.arange(token_count, dtype=jnp.int32)
    allowed = (segment[:, None] == segment[None, :]) & (place[None, :] <= place[:, None])
    tables = rotary_tables(positions, head_dim) + (jnp.where(allowed, 0.0, MASKED).astype(F32),)

    shard = lax.axis_index("z") * PLANE + lax.axis_index("p")

    def placed(part):
        whole = jnp.zeros((part.shape[0] * shards,), part.dtype)
        return lax.dynamic_update_slice(whole, part, (shard * part.shape[0],)).reshape(-1, LANE)

    vec = jnp.concatenate(
        [placed(x) for x in (norm_attn, norm_mlp, b_query[0], b_key[0], b_value[0])], 0
    )
    aset_all, vec_sum, wg, wu, wd, grad_rows, h1_all, *heads, residual, mlp_low = gather_all(
        jnp.concatenate([w_query, w_key, w_value, w_out.T], 1),
        vec,
        w_gate,
        w_up,
        w_down.T,
        out_grad.astype(BF),
        hidden_in,
        *tables,
        quarters,
        part_width,
    )
    y_half, dh2, *mlp_grads = mlp_all(
        mlp_low,
        grad_rows.reshape(quarters, token_count, width),
        *[w.reshape(width, part_width) for w in (wg, wu, wd)],
        hidden_width,
    )
    small_total, attn_part, block_out, grad_in, *quarter_grads = reduce_all(
        quarters,
        [g.reshape(shards, depth, part_width) for g in mlp_grads],
        y_half,
        dh2,
        residual,
        out_grad,
        hidden_in,
        h1_all,
        heads,
        aset_all,
        vec_sum,
        tables,
    )

    def whole_rows(parts):
        taken = []
        for index in range(quarters):
            skip = max(0, index * part_width - (hidden_width - part_width))
            if skip < part_width:
                taken.append(parts[index][:, skip:])
        return jnp.concatenate(taken, 1).astype(F32)

    grad_w_gate, grad_w_up, grad_w_down = [whole_rows(parts) for parts in quarter_grads]
    if copies > 1:
        small_total = lax.psum(small_total, "o")
        attn_part, grad_w_gate, grad_w_up, grad_w_down = [
            lax.psum_scatter(x, "o", scatter_dimension=0, tiled=True)
            for x in (attn_part, grad_w_gate, grad_w_up, grad_w_down)
        ]
    small_total = small_total.reshape(lanes, -1)
    gain_total = jnp.sum(small_total[:, : 2 * width], 0).reshape(2, width)
    bias_total = small_total[:, 2 * width :]
    return (
        block_out,
        grad_in,
        gain_total[0],
        attn_part[:, :query_width],
        bias_total[:, :query_width],
        attn_part[:, query_width : query_width + head_dim],
        bias_total[:, query_width : query_width + head_dim],
        attn_part[:, query_width + head_dim : query_width + 2 * head_dim],
        bias_total[:, query_width + head_dim :],
        attn_part[:, query_width + 2 * head_dim :].T,
        gain_total[1],
        grad_w_gate,
        grad_w_up,
        grad_w_down.T,
    )


def solution(mesh):
    shards = mesh.shape["dp"]
    copies = max(1, shards // (PLANE * PLANE))
    shape = (shards // (PLANE * copies), PLANE, copies, mesh.shape["head"])
    split = jax.sharding.Mesh(mesh.devices.reshape(shape), DP + ("head",))
    rows = P(DP + ("head",), None)
    deep = P(DP, "head")
    wide = P("head", DP)
    return jax.shard_map(
        local,
        mesh=split,
        in_specs=(
            rows,
            P(DP, None),
            P(DP),
            deep,
            wide,
            deep,
            wide,
            deep,
            wide,
            wide,
            P(DP),
            deep,
            deep,
            wide,
            rows,
        ),
        out_specs=(
            rows,
            rows,
            P(),
            deep,
            P(),
            deep,
            P(),
            deep,
            P(),
            wide,
            P(),
            deep,
            deep,
            wide,
        ),
        check_vma=False,
    )
```

```python
import functools
import math

import jax
import jax.numpy as jnp
from jax import lax
from jax.experimental import pallas as pl
from jax.experimental.pallas import tpu as pltpu
from jax.sharding import PartitionSpec as P

NORM_EPS = 1e-06
ROPE_BASE = 1000000.0
MASKED = -1e30
MESH_ID = pl.DeviceIdType.MESH
PLANE = 4
DP = ("z", "p", "o")
LANE = 128
TILE = 256
BF = jnp.bfloat16
F32 = jnp.float32


def layout(lengths_row, token_count):
    row_ends = jnp.stack([jnp.sum(lengths_row[: i + 1]) for i in range(lengths_row.shape[0])])
    places = jnp.arange(token_count, dtype=jnp.int32)
    passed = (places[:, None] >= row_ends[None, :]).astype(jnp.int32)
    segment = jnp.sum(passed, axis=1)
    offset = jnp.sum(passed * lengths_row[None, :], axis=1)
    return (segment, places - offset)


def rotary_tables(positions, head_dim):
    half_dim = head_dim // 2
    frequency = jnp.exp(
        jnp.arange(half_dim, dtype=F32) * (-2.0 * math.log(ROPE_BASE) / head_dim)
    )
    angles = positions.astype(F32)[:, None] * frequency[None, :]
    cosine = jnp.cos(angles)
    sine_tab = jnp.sin(angles)
    return (jnp.concatenate([cosine, cosine], -1), jnp.concatenate([-sine_tab, sine_tab], -1))


def dot(left, right):
    return jnp.dot(left, right, preferred_element_type=F32)


def dot_last(left, right):
    return lax.dot_general(left, right, (((1,), (1,)), ((), ())), preferred_element_type=F32)


def dot_first(left, right):
    return lax.dot_general(left, right, (((0,), (0,)), ((), ())), preferred_element_type=F32)


def flipped(index, mask):
    bit = 1
    while bit <= mask:
        if mask & bit:
            index = index + bit - 2 * bit * lax.rem(lax.div(index, bit), 2)
        bit *= 2
    return index


def moved(index, other, count):
    total, bit = 0, 1
    while bit < count:
        a, b = lax.rem(lax.div(index, bit), 2), lax.rem(lax.div(other, bit), 2)
        total = total + bit * (a + b - 2 * a * b)
        bit *= 2
    return total


def spot(z, p, c):
    return {"z": z, "p": p, "head": c}


def here():
    return (lax.axis_index("z"), lax.axis_index("p"), lax.axis_index("head"))


def greet(peers):
    bar = pltpu.get_barrier_semaphore()
    for peer in peers:
        pl.semaphore_signal(bar, inc=1, device_id=peer, device_id_type=MESH_ID)
    pl.semaphore_wait(bar, len(peers))


def push(src, dst, ssem, rsem, peer):
    copy = pltpu.make_async_remote_copy(
        src_ref=src, dst_ref=dst, send_sem=ssem, recv_sem=rsem,
        device_id=peer, device_id_type=MESH_ID,
    )
    copy.start()
    return copy


def landed(ref, sem):
    pltpu.make_async_copy(ref, ref, sem).wait()


def line_of(table, start, count):
    return jnp.concatenate([table[i : i + 1, :] for i in range(start, start + count)], axis=1)


def wide_mean(value):
    return jnp.mean(value, axis=-1, keepdims=True)


def softmax_of(query, key, mask_bias):
    scores = dot_last(query, key) * (1.0 / math.sqrt(query.shape[-1])) + mask_bias
    top = jnp.max(scores, axis=-1, keepdims=True)
    exp_scores = jnp.exp(scores - top)
    return exp_scores / jnp.sum(exp_scores, axis=-1, keepdims=True)


class line_spread:
    def __init__(self, quarters, z, own, slot, g_send, g_recv, f_send, f_recv, at, pair):
        self.quarters, self.z, self.own, self.slot = (quarters, z, own, slot)
        self.g_send, self.g_recv, self.f_send, self.f_recv = (g_send, g_recv, f_send, f_recv)
        self.at, self.pair = (at, pair)

    def inside(self, zz):
        return (zz >= 0) & (zz < self.quarters)

    def begin(self):
        for i, side in enumerate((-1, 1)):
            to = self.z + side

            @pl.when(self.inside(to))
            def _():
                push(
                    self.own, self.slot(to, self.z), self.g_send.at[self.quarters + i],
                    self.g_recv.at[self.z], self.at(to),
                )

    def pass_on(self, distance):
        for side in (-1, 1):
            src = self.z + side * distance
            to = self.z - side

            @pl.when(self.inside(src))
            def _():
                ref = self.slot(self.z, src)
                landed(ref, self.g_recv.at[src])

                @pl.when(self.inside(to))
                def _():
                    push(ref, self.slot(to, src), self.g_send.at[src], self.g_recv.at[src], self.at(to))

                push(ref, ref, self.f_send.at[src], self.f_recv.at[src], self.pair)

    def end(self):
        for i, side in enumerate((-1, 1)):

            @pl.when(self.inside(self.z + side))
            def _():
                landed(self.own, self.g_send.at[self.quarters + i])

        for src in range(self.quarters):
            landed(self.own, self.f_send.at[src])
            right, left = (src < self.z, src > self.z)

            @pl.when((right & self.inside(self.z + 1)) | (left & self.inside(self.z - 1)))
            def _():
                landed(self.own, self.g_send.at[src])


def gather_kernel(
    quarters,
    part_cols,
    aset,
    vec,
    gate,
    up,
    down,
    out_grad,
    hidden,
    cosine,
    sine_tab,
    mask_bias,
    aset_out,
    vec_sum,
    gate_all,
    up_all,
    down_all,
    grad_all,
    h1_keep,
    q_keep,
    k_keep,
    v_keep,
    o_keep,
    r1_keep,
    h2_keep,
    aset_all,
    grad,
    h1_all,
    q_out,
    k_out,
    v_out,
    o_out,
    r1_out,
    h2_out,
    vec_all,
    halves,
    pair_out,
    pair_in,
    a_send,
    a_recv,
    m_send,
    m_recv,
    s_send,
    s_recv,
    g_send,
    g_recv,
    f_send,
    f_recv,
    p_send,
    p_recv,
    l_sem,
    k_sem,
):
    z, p, c = here()
    dp = z * PLANE + p
    units = gate.shape[1]
    shards, depth = aset_all.shape[:2]
    rows, width = hidden.shape
    head_dim = cosine.shape[1]
    query_width = q_out.shape[1]
    qkv_width = query_width + 2 * head_dim
    group_heads = query_width // head_dim
    wide = width // LANE

    def at(zz, pp):
        return spot(zz, pp, c)

    pair = spot(z, p, 1 - c)
    masks = [(kz, kp) for kz in range(quarters) for kp in range(PLANE) if kz or kp]
    greet([at(flipped(z, kz), flipped(p, kp)) for kz, kp in masks] + [pair])

    px, py = flipped(p, 1), flipped(p, 2)
    sent = []
    grad[...] = out_grad[...].astype(BF)

    def send(*args):
        sent.append(push(*args))

    def cols_of(weight, quarter):
        first = jnp.minimum(quarter * part_cols, units - part_cols)
        return weight.at[:, pl.ds(pl.multiple_of(first, LANE), part_cols)]

    sets = [(aset_all, lambda zz: aset, a_send, a_recv)] + [
        (whole, functools.partial(cols_of, weight), m_send.at[i], m_recv.at[i])
        for i, (whole, weight) in enumerate(((gate_all, gate), (up_all, up), (down_all, down)))
    ]

    def line(s, k):
        whole, part, ss, rs = sets[s]
        zz = flipped(z, k)
        send(part(zz), whole.at[dp], ss.at[k, 0], rs.at[k, 0], at(zz, p))

    def came(s, k, role):
        whole, _, _, rs = sets[s]
        landed(whole.at[flipped(z, k) * PLANE + flipped(p, role)], rs.at[k, role])

    def fan(s, k):
        whole, part, ss, rs = sets[s]
        slot = flipped(z, k) * PLANE + p
        src = whole.at[slot] if k else part(z)
        if k:
            came(s, k, 0)
        send(src, whole.at[slot], ss.at[k, 1], rs.at[k, 1], at(z, px))
        send(src, whole.at[slot], ss.at[k, 2], rs.at[k, 2], at(z, py))

    def relay(s, k):
        whole, _, ss, rs = sets[s]
        role = 1 if k % 2 == 0 else 2
        came(s, k, role)
        slot = flipped(z, k) * PLANE + flipped(p, role)
        to = py if role == 1 else px
        send(whole.at[slot], whole.at[slot], ss.at[k, 3], rs.at[k, 3], at(z, to))

    def rest(s, k):
        came(s, k, 2 if k % 2 == 0 else 1)
        came(s, k, 3)

    others = range(1, quarters)
    for n, (kz, kp) in enumerate(masks):
        send(vec, vec_all.at[dp], s_send.at[n], s_recv.at[n], at(flipped(z, kz), flipped(p, kp)))
    local = [
        pltpu.make_async_copy(vec, vec_all.at[dp], l_sem.at[0]),
        pltpu.make_async_copy(aset, aset_all.at[dp], l_sem.at[1]),
        pltpu.make_async_copy(cols_of(gate, z), gate_all.at[dp], l_sem.at[2]),
        pltpu.make_async_copy(cols_of(up, z), up_all.at[dp], l_sem.at[3]),
        pltpu.make_async_copy(cols_of(down, z), down_all.at[dp], l_sem.at[4]),
        pltpu.make_async_copy(grad, grad_all.at[0, c], l_sem.at[5]),
    ]
    fan(0, 0)
    for k in others:
        line(0, k)
    for s in (1, 2, 3):
        for k in others:
            line(s, k)
    for copy in local:
        copy.start()
    push(grad, grad_all.at[0, c], f_send.at[z], f_recv.at[z], pair)
    spread = line_spread(
        quarters, z, grad, lambda zz, src: grad_all.at[moved(zz, src, quarters), c],
        g_send, g_recv, f_send, f_recv, lambda zz: at(zz, p), pair,
    )
    spread.begin()
    fan(1, 0)

    local[0].wait()
    for n, (kz, kp) in enumerate(masks):
        landed(vec_all.at[flipped(z, kz) * PLANE + flipped(p, kp)], s_recv.at[n])
    total = vec_all[0].astype(F32)
    for i in range(1, shards):
        total = total + vec_all[i].astype(F32)
    vec_sum[...] = total
    x = hidden[...]
    normed = x * lax.rsqrt(wide_mean(x * x) + NORM_EPS) * line_of(total, 0, wide)
    h1_all[c] = normed.astype(BF)
    send(h1_all.at[c], h1_all.at[c], p_send.at[0], p_recv.at[0], pair)

    relay(0, 0)
    for k in others:
        fan(0, k)
    fan(2, 0)
    fan(3, 0)
    for k in others:
        relay(0, k)
    relay(1, 0)
    local[1].wait()
    for k in range(quarters):
        rest(0, k)
    landed(h1_all.at[1 - c], p_recv.at[0])
    kept = []

    def keep(src, dst):
        copy = pltpu.make_async_copy(src, dst, k_sem.at[len(kept)])
        copy.start()
        kept.append(copy)

    keep(aset_all, aset_out)
    keep(h1_all, h1_keep)

    def project(n):
        cols = slice(n * TILE, (n + 1) * TILE)
        weight = aset_all[:, :, cols].reshape(width, TILE)
        out = dot(h1_all[...].reshape(2 * rows, width), weight)
        out = out + line_of(vec_sum[...], 2 * wide + n * TILE // LANE, TILE // LANE)
        for j in range(TILE // head_dim):
            head = n * TILE // head_dim + j
            u = out[:, j * head_dim : (j + 1) * head_dim]
            if head <= group_heads:
                u = u * cosine[...] + pltpu.roll(u, head_dim // 2, 1) * sine_tab[...]
            u = u.astype(BF)
            if head < group_heads:
                q_out[:, head * head_dim : (head + 1) * head_dim] = u
            elif head == group_heads:
                k_out[...] = u
            else:
                v_out[...] = u

    def attend(head):
        cols = slice(head * head_dim, (head + 1) * head_dim)
        probs = softmax_of(q_out[:, cols], k_out[...], mask_bias[...])
        o_out[:, cols] = dot(probs.astype(BF), v_out[...]).astype(BF)

    def leave(i):
        half = shards // 2
        weight = aset_all[i * half : (i + 1) * half, :, qkv_width:].reshape(width // 2, query_width)
        out = dot_last(o_out[...], weight)
        cols = slice(i * width // 2, (i + 1) * width // 2)
        halves[0, :, cols] = out[:rows]
        halves[1, :, cols] = out[rows:]

    def swap():
        for src, dst in ((q_out, q_keep), (k_out, k_keep), (v_out, v_keep), (o_out, o_keep)):
            keep(src, dst)
        pair_out[...] = halves[1 - c].astype(BF)
        send(pair_out, pair_in, p_send.at[1], p_recv.at[1], pair)

    def enter():
        landed(pair_in, p_recv.at[1])
        residual = hidden[...] + halves[c] + pair_in[...].astype(F32)
        r1_out[...] = residual
        gain = line_of(vec_sum[...], wide, wide)
        keep(r1_out, r1_keep)
        h2_out[...] = (residual * lax.rsqrt(wide_mean(residual * residual) + NORM_EPS) * gain).astype(BF)
        keep(h2_out, h2_keep)

    work = [functools.partial(project, n) for n in range(qkv_width // TILE)]
    work += [functools.partial(attend, head) for head in range(group_heads)]
    work += [functools.partial(leave, i) for i in range(2)] + [swap, enter]
    moves = [functools.partial(fan, 1, k) for k in others]
    moves += [functools.partial(relay, s, 0) for s in (2, 3)]
    for k in others:
        moves += [functools.partial(fan, 2, k), functools.partial(relay, 1, k)]
    moves.append(functools.partial(spread.pass_on, 1))
    for k in others:
        moves += [functools.partial(fan, 3, k), functools.partial(relay, 2, k)]
    moves.append(functools.partial(spread.pass_on, 2))
    moves += [functools.partial(relay, 3, k) for k in others]
    for i in range(max(len(work), len(moves))):
        if i < len(moves):
            moves[i]()
        if i < len(work):
            work[i]()
    spread.pass_on(quarters - 1)
    for src in range(quarters):
        landed(grad_all.at[moved(z, src, quarters), 1 - c], f_recv.at[src])
    spread.end()
    for s in (1, 2, 3):
        for k in range(quarters):
            rest(s, k)
    for copy in local[2:] + kept:
        copy.wait()
    for copy in sent:
        copy.wait_send()


def gather_all(aset, vec, gate, up, down, out_grad, hidden, cosine, sine_tab, mask_bias, quarters, part_cols):
    shards = quarters * PLANE
    depth = aset.shape[0]
    head_dim = cosine.shape[1]
    query_width = (aset.shape[1] - 2 * head_dim) // 2
    rows, width = hidden.shape
    dma = pltpu.SemaphoreType.DMA
    hbm = pl.BlockSpec(memory_space=pltpu.HBM)
    vmem = pl.BlockSpec(memory_space=pltpu.VMEM)
    shape = jax.ShapeDtypeStruct
    part = shape((shards, depth, part_cols), BF)
    kept = (
        ((2, rows, width), BF),
        ((2 * rows, query_width), BF),
        ((2 * rows, head_dim), BF),
        ((2 * rows, head_dim), BF),
        ((2 * rows, query_width), BF),
        ((rows, width), F32),
        ((rows, width), BF),
    )
    return pl.pallas_call(
        functools.partial(gather_kernel, quarters, part_cols),
        out_shape=(
            shape((shards,) + aset.shape, BF),
            shape(vec.shape, F32),
            part,
            part,
            part,
            shape((quarters, 2, rows, width), BF),
        )
        + tuple(shape(*entry) for entry in kept),
        in_specs=[hbm] * 5 + [vmem] * 5,
        out_specs=[hbm, vmem] + [hbm] * 11,
        scratch_shapes=[pltpu.VMEM((shards,) + aset.shape, BF), pltpu.VMEM((rows, width), BF)]
        + [pltpu.VMEM(*entry) for entry in kept]
        + [
            pltpu.VMEM((shards,) + vec.shape, BF),
            pltpu.VMEM((2, rows, width), F32),
            pltpu.VMEM((rows, width), BF),
            pltpu.VMEM((rows, width), BF),
            dma((quarters, 4)),
            dma((quarters, 4)),
            dma((3, quarters, 4)),
            dma((3, quarters, 4)),
            dma((shards - 1,)),
            dma((shards - 1,)),
            dma((quarters + 2,)),
            dma((quarters,)),
            dma((quarters,)),
            dma((quarters,)),
            dma((2,)),
            dma((2,)),
            dma((6,)),
            dma((8,)),
        ],
        compiler_params=pltpu.CompilerParams(
            collective_id=0, has_side_effects=True, vmem_limit_bytes=48 * 2**20
        ),
    )(aset, vec, gate, up, down, out_grad, hidden, cosine, sine_tab, mask_bias)


def mlp_kernel(
    quarters,
    hidden,
    own,
    grads,
    gate,
    up,
    down,
    y_out,
    d_out,
    gate_out,
    up_out,
    down_out,
    h_all,
    g_all,
    w_all,
    act,
    d_gate,
    d_up,
    y_part,
    d_part,
    y_slot,
    d_slot,
    d_line,
    h_send,
    h_recv,
    hp_send,
    hp_recv,
    y_send,
    y_recv,
    d_send,
    d_recv,
    l_send,
    l_recv,
    load_sem,
    out_sem,
):
    z, p, c = here()
    pair = spot(z, p, 1 - c)
    rows, width = own.shape
    part_cols = gate.shape[1]
    padded = w_all.shape[2]
    tiles = padded // TILE

    def half(k, lane):
        return h_all.at[k, pl.ds(pl.multiple_of(lane * rows, 16), rows)]

    loads = [
        pltpu.make_async_copy(w, w_all.at[i, :, pl.ds(0, part_cols)], load_sem.at[i])
        for i, w in enumerate((gate, up, down))
    ] + [pltpu.make_async_copy(grads, g_all, load_sem.at[3]), pltpu.make_async_copy(own, half(0, c), load_sem.at[4])]
    for copy in loads:
        copy.start()
    greet([spot(flipped(z, k), p, c) for k in range(1, quarters)] + [pair])
    push(own, half(0, c), hp_send.at[z], hp_recv.at[z], pair)
    spread = line_spread(
        quarters, z, own, lambda zz, src: half(moved(zz, src, quarters), c),
        h_send, h_recv, hp_send, hp_recv, lambda zz: spot(zz, p, c), pair,
    )
    spread.begin()
    if padded > part_cols:
        for i in range(3):
            w_all[i, :, part_cols:] = jnp.zeros((width, padded - part_cols), w_all.dtype)
    first = jnp.minimum(z * part_cols, hidden - part_cols)
    skip = z * part_cols - first
    for copy in loads:
        copy.wait()

    def finish(k):
        mine, other = (y_part.at[k, c], y_slot.at[k])
        landed(other, y_recv.at[k])
        other[...] = (other[...].astype(F32) + mine[...].astype(F32)).astype(other.dtype)
        pltpu.make_async_copy(other, y_out.at[k], out_sem.at[0, k]).start()
        mine, other = (d_part.at[k, c], d_slot.at[k])
        landed(other, d_recv.at[k])
        other[...] = (other[...].astype(F32) + mine[...].astype(F32)).astype(other.dtype)

        @pl.when(k > 0)
        def _():
            push(other, d_line.at[k], l_send.at[k], l_recv.at[k], spot(moved(z, k, quarters), p, c))

    edge = (z == 0) | (z == quarters - 1)

    def offset(step):
        return jnp.where(edge | (step == 0), step, quarters - step)

    def block(step, carry):
        k = offset(step)

        @pl.when(step > 0)
        def _():
            spread.pass_on(step)

        src = moved(z, k, quarters)
        landed(half(k, 1 - c), hp_recv.at[src])

        def units(n, carry):
            cols = pl.ds(pl.multiple_of(n * TILE, TILE), TILE)
            h = h_all[k]
            g = jnp.dot(h, w_all[0, :, cols], preferred_element_type=F32)
            u = jnp.dot(h, w_all[1, :, cols], preferred_element_type=F32)
            da = jnp.dot(g_all[k], w_all[2, :, cols], preferred_element_type=F32)
            column = n * TILE + lax.broadcasted_iota(jnp.int32, (1, TILE), 1)
            ok = column >= skip
            g = jnp.where(ok, g, 0.0)
            u = jnp.where(ok, u, 0.0)
            s = 1.0 / (1.0 + jnp.exp(-g))
            sg = g * s
            act[k, :, cols] = (sg * u).astype(BF)
            d_gate[k, :, cols] = (da * u * s * (1.0 + g * (1.0 - s))).astype(BF)
            d_up[k, :, cols] = (da * sg).astype(BF)
            return carry

        lax.fori_loop(0, tiles, units, 0, unroll=True)

        @pl.when(step > 0)
        def _():
            finish(offset(step - 1))

        def model(n, carry):
            cols = pl.ds(pl.multiple_of(n * TILE, TILE), TILE)

            def back(left, index):
                return lax.dot_general(
                    left[k], w_all[index, cols, :], (((1,), (1,)), ((), ())),
                    preferred_element_type=F32,
                )

            y = back(act, 2).astype(BF)
            d = (back(d_gate, 0) + back(d_up, 1)).astype(BF)
            for lane in range(2):
                y_part[k, lane, :, cols] = y[lane * rows : (lane + 1) * rows]
                d_part[k, lane, :, cols] = d[lane * rows : (lane + 1) * rows]
            return carry

        lax.fori_loop(0, width // TILE, model, 0)
        push(y_part.at[k, 1 - c], y_slot.at[k], y_send.at[k], y_recv.at[k], pair)
        push(d_part.at[k, 1 - c], d_slot.at[k], d_send.at[k], d_recv.at[k], pair)
        return carry

    lax.fori_loop(0, quarters, block, 0)
    finish(offset(quarters - 1))

    outs = (gate_out, up_out, down_out)

    def weight(n, carry):
        cols = pl.ds(pl.multiple_of(n * TILE, TILE), TILE)
        for i, (left, right) in enumerate(((h_all, d_gate), (h_all, d_up), (g_all, act))):
            total = dot_first(
                left[:, :, cols].reshape(quarters * 2 * rows, TILE),
                right[...].reshape(quarters * 2 * rows, padded),
            )
            w_all[i, cols, :] = total.astype(BF)
            pltpu.make_async_copy(
                w_all.at[i, cols, pl.ds(0, part_cols)], outs[i].at[cols, :], out_sem.at[1 + i, n]
            ).start()
        return carry

    lax.fori_loop(0, width // TILE, weight, 0)
    total = d_slot[0].astype(F32)
    for k in range(1, quarters):
        landed(d_line.at[k], l_recv.at[k])
        total = total + d_line[k].astype(F32)
    d_out[...] = total
    for n in range(width // TILE):
        for i in range(3):
            tile = w_all.at[i, pl.ds(n * TILE, TILE), pl.ds(0, part_cols)]
            pltpu.make_async_copy(tile, outs[i].at[pl.ds(n * TILE, TILE), :], out_sem.at[1 + i, n]).wait()
    spread.end()
    for k in range(quarters):
        pltpu.make_async_copy(y_slot.at[k], y_out.at[k], out_sem.at[0, k]).wait()
        landed(y_part.at[k, 1 - c], y_send.at[k])
        landed(d_part.at[k, 1 - c], d_send.at[k])
        if k:
            landed(d_slot.at[k], l_send.at[k])


def mlp_all(own, grads, gate, up, down, hidden):
    bf = jnp.bfloat16
    quarters, block_rows, width = grads.shape
    part_cols = gate.shape[1]
    padded = -(-part_cols // TILE) * TILE
    rows = own.shape[0]
    dma = pltpu.SemaphoreType.DMA
    hbm = pl.BlockSpec(memory_space=pltpu.HBM)
    vmem = pl.BlockSpec(memory_space=pltpu.VMEM)
    grad_w = jax.ShapeDtypeStruct((width, part_cols), bf)
    steps = max(quarters, width // TILE)
    return pl.pallas_call(
        functools.partial(mlp_kernel, quarters, hidden),
        out_shape=(
            jax.ShapeDtypeStruct((quarters, rows, width), bf),
            jax.ShapeDtypeStruct((rows, width), F32),
            grad_w,
            grad_w,
            grad_w,
        ),
        in_specs=[hbm] * 5,
        out_specs=[hbm, vmem, hbm, hbm, hbm],
        scratch_shapes=[
            pltpu.VMEM((quarters, block_rows, width), bf),
            pltpu.VMEM((quarters, block_rows, width), bf),
            pltpu.VMEM((3, width, padded), bf),
            pltpu.VMEM((quarters, block_rows, padded), bf),
            pltpu.VMEM((quarters, block_rows, padded), bf),
            pltpu.VMEM((quarters, block_rows, padded), bf),
            pltpu.VMEM((quarters, 2, rows, width), bf),
            pltpu.VMEM((quarters, 2, rows, width), bf),
            pltpu.VMEM((quarters, rows, width), bf),
            pltpu.VMEM((quarters, rows, width), bf),
            pltpu.VMEM((quarters, rows, width), bf),
        ]
        + [dma((quarters + 2,))]
        + [dma((quarters,))] * 9
        + [dma((5,)), dma((4, steps))],
        compiler_params=pltpu.CompilerParams(
            collective_id=2, has_side_effects=True, vmem_limit_bytes=60 * 2**20
        ),
    )(own, grads, gate, up, down)


AHEAD = 2
LAG = 1
PIECES = 2
LINE_STEPS = (4, 9)


INPUTS = 15


def reduce_kernel(quarters, gate, up, down, *refs):
    given, refs = (refs[:INPUTS], refs[INPUTS:])
    (small_sum, attn_sum, block_out, grad_in, gate_out, up_out, down_out), refs = (refs[:7], refs[7:])
    (
        small,
        small_all,
        staged,
        attn_slots,
        mlp_slots,
        mlp_own,
        attn_line,
        y_line,
        attn_grads,
        da_all,
        dr1,
        do_all,
        dqkv,
        dk_sum,
        dv_sum,
        halves,
        pair_out,
        pair_in,
    ), refs = (refs[:18], refs[18:])
    taken, refs = (refs[:INPUTS], refs[INPUTS:])
    (
        y_half,
        d_sum,
        r1,
        out_grad,
        vec_sum,
        cosine,
        sine_tab,
        mask_bias,
        aset_all,
        q_in,
        k_in,
        v_in,
        hidden,
        h1_all,
        o_in,
    ) = taken
    (
        t_send,
        t_recv,
        z_send,
        z_recv,
        s_send,
        s_recv,
        y_send,
        y_recv,
        p_send,
        p_recv,
        l_sem,
        own_sem,
        in_sem,
    ) = refs
    loads = [pltpu.make_async_copy(src, dst, in_sem.at[i]) for i, (src, dst) in enumerate(zip(given, taken))]

    def need(count):
        while len(loads) > INPUTS - count:
            loads.pop(0).wait()

    z, p, c = here()
    dp = z * PLANE + p
    pair = spot(z, p, 1 - c)
    shards, depth, attn_width = aset_all.shape
    rows, width = r1.shape
    head_dim = cosine.shape[1]
    query_width = q_in.shape[1]
    qkv_width = query_width + 2 * head_dim
    group_heads = query_width // head_dim
    wide = width // LANE
    others = range(1, quarters)
    scale = 1.0 / math.sqrt(head_dim)
    sources = (attn_grads, gate, up, down)
    outs = (None, gate_out, up_out, down_out)

    def source(s, k, kp):
        return sources[s].at[flipped(z, k) * PLANE + flipped(p, kp)]

    ks = list(others) + [0]
    units = [(s, k) for i in range(0, quarters, 2) for s in (1, 2, 3) for k in ks[i : i + 2]]
    for s, k in units:
        for i, kp in enumerate((0, 2 - k % 2)):
            pltpu.make_async_copy(source(s, k, kp), mlp_own.at[s - 1, k, i], own_sem.at[s - 1, k, i]).start()
    for copy in loads:
        copy.start()
    masks = [(kz, kp) for kz in range(quarters) for kp in range(PLANE) if kz or kp]
    greet([spot(flipped(z, kz), flipped(p, kp), c) for kz, kp in masks] + [pair])
    sent = []
    local = []

    def send(*args):
        sent.append(push(*args))

    side = [spot(z, flipped(p, 1), c), spot(z, flipped(p, 2), c)]

    def slots(s, k, role):
        return attn_slots.at[k, role] if s == 0 else mlp_slots.at[s - 1, k, role]

    def term(s, k, i):
        if s == 0:
            return source(s, k, (0, 2 - k % 2)[i])
        return mlp_own.at[s - 1, k, i]

    def ready(s, k, i):
        if s:
            landed(mlp_own.at[s - 1, k, i], own_sem.at[s - 1, k, i])

    def first(s, k):
        way = k % 2
        send(source(s, k, 3), slots(s, k, 0), t_send.at[s, k, 0], t_recv.at[s, k, 0], side[way])
        send(source(s, k, 1 + way), slots(s, k, 1), t_send.at[s, k, 1], t_recv.at[s, k, 1], side[way])

    def relay(s, k):
        slot = slots(s, k, 0)
        ready(s, k, 1)
        landed(slot, t_recv.at[s, k, 0])
        slot[...] = (slot[...].astype(F32) + term(s, k, 1)[...].astype(F32)).astype(BF)
        send(slot, slots(s, k, 2), t_send.at[s, k, 2], t_recv.at[s, k, 2], side[1 - k % 2])

    def last(s, k):
        one, two = (slots(s, k, 1), slots(s, k, 2))
        ready(s, k, 0)
        landed(one, t_recv.at[s, k, 1])
        landed(two, t_recv.at[s, k, 2])
        total = term(s, k, 0)[...].astype(F32) + one[...].astype(F32) + two[...].astype(F32)
        one[...] = total.astype(BF)
        if s == 0:
            if k:
                send(one, attn_line.at[k], z_send.at[s, k], z_recv.at[s, k], spot(flipped(z, k), p, c))
        elif k:
            send(one, outs[s].at[z], z_send.at[s, k], z_recv.at[s, k], spot(flipped(z, k), p, c))
        else:
            copy = pltpu.make_async_copy(one, outs[s].at[z], l_sem.at[s])
            copy.start()
            local.append(copy)

    def note(value, start):
        for i in range(value.shape[1] // LANE):
            small[start + i : start + i + 1, :] = value[:, i * LANE : (i + 1) * LANE]

    def line_terms(step):
        for way, side in enumerate((1, -1)):
            here_z = step if way == 0 else quarters - 1 - step
            targets = range(quarters - 1, here_z, -1) if way == 0 else range(here_z)

            @pl.when(z == here_z)
            def _():
                for target in targets:
                    slot, mine = (y_line.at[way, target], y_half.at[here_z ^ target])
                    if step:
                        landed(slot, y_recv.at[way, target])
                        slot[...] = (slot[...].astype(F32) + mine[...].astype(F32)).astype(BF)
                    push(
                        slot if step else mine, y_line.at[way, target], y_send.at[way, target],
                        y_recv.at[way, target], spot(here_z + side, p, c),
                    )

    def line_total():
        total = r1[...] + y_half[0].astype(F32)
        block_out[...] = total
        for way, first_z in ((0, 0), (1, quarters - 1)):

            @pl.when(z != first_z)
            def _():
                landed(y_line.at[way, z], y_recv.at[way, z])
                block_out[...] += y_line[way, z].astype(F32)

    def line_end():
        for at in range(quarters):

            @pl.when(z == at)
            def _():
                for target in range(quarters):
                    if target != at:
                        way = 0 if target > at else 1
                        landed(y_half.at[0], y_send.at[way, target])

    def norm_back():
        need(5)
        residual, dh2 = (r1[...], d_sum[...])
        rho = lax.rsqrt(wide_mean(residual * residual) + NORM_EPS)
        n = residual * rho
        inner = dh2 * line_of(vec_sum[...], wide, wide)
        note(jnp.sum(dh2 * n, axis=0, keepdims=True), wide)
        total = out_grad[...] + rho * (inner - n * wide_mean(inner * n))
        dr1[...] = total
        da_all[c] = total.astype(BF)
        send(da_all.at[c], da_all.at[c], p_send.at[0], p_recv.at[0], pair)

    def heads_back(n):
        if n == 0:
            need(INPUTS)
            landed(da_all.at[1 - c], p_recv.at[0])
        cols = slice(n * TILE, (n + 1) * TILE)
        weight = aset_all[:, :, qkv_width + n * TILE : qkv_width + (n + 1) * TILE]
        do_all[:, cols] = dot(da_all[...].reshape(2 * rows, width), weight.reshape(width, TILE)).astype(BF)

    def unrotate(value):
        return value * cosine[...] - pltpu.roll(value, head_dim // 2, 1) * sine_tab[...]

    def attend_back(head):
        cols = slice(head * head_dim, (head + 1) * head_dim)
        query, grad = (q_in[:, cols], do_all[:, cols])
        probs = softmax_of(query, k_in[...], mask_bias[...])
        grad_probs = dot_last(grad, v_in[...])
        centre = jnp.sum(grad_probs * probs, axis=-1, keepdims=True)
        grad_scores = (probs * (grad_probs - centre) * scale).astype(BF)
        dqkv[:, cols] = unrotate(dot(grad_scores, k_in[...])).astype(BF)
        key_term = dot_first(grad_scores, query)
        value_term = dot_first(probs.astype(BF), grad)
        dk_sum[...] = key_term if head == 0 else dk_sum[...] + key_term
        dv_sum[...] = value_term if head == 0 else dv_sum[...] + value_term

    def keys_back():
        dqkv[:, query_width : query_width + head_dim] = unrotate(dk_sum[...]).astype(BF)
        dqkv[:, query_width + head_dim :] = dv_sum[...].astype(BF)
        note(jnp.sum(dqkv[...].astype(F32), axis=0, keepdims=True), 2 * wide)

    def inputs_back(i):
        half = shards // 2
        weight = aset_all[i * half : (i + 1) * half, :, :qkv_width].reshape(width // 2, qkv_width)
        out = dot_last(dqkv[...], weight)
        cols = slice(i * width // 2, (i + 1) * width // 2)
        halves[0, :, cols] = out[:rows]
        halves[1, :, cols] = out[rows:]
        if i:
            pair_out[...] = halves[1 - c].astype(BF)
            send(pair_out, pair_in, p_send.at[1], p_recv.at[1], pair)

    def weights_back(i):
        cols = slice(i * 4 * depth, (i + 1) * 4 * depth)
        blocks = slice(i * 4, (i + 1) * 4)
        left = h1_all[:, :, cols].reshape(2 * rows, 4 * depth)
        attn_grads[blocks, :, :qkv_width] = (
            dot_first(left, dqkv[...]).astype(BF).reshape(4, depth, qkv_width)
        )
        left = da_all[:, :, cols].reshape(2 * rows, 4 * depth)
        attn_grads[blocks, :, qkv_width:] = (
            dot_first(left, o_in[...]).astype(BF).reshape(4, depth, query_width)
        )

    def leave():
        landed(pair_in, p_recv.at[1])
        x = hidden[...]
        dh1 = halves[c] + pair_in[...].astype(F32)
        rho = lax.rsqrt(wide_mean(x * x) + NORM_EPS)
        n = x * rho
        inner = dh1 * line_of(vec_sum[...], 0, wide)
        note(jnp.sum(dh1 * n, axis=0, keepdims=True), 0)
        grad_in[...] = dr1[...] + rho * (inner - n * wide_mean(inner * n))
        for n, (kz, kp) in enumerate(masks):
            peer = spot(flipped(z, kz), flipped(p, kp), c)
            send(small, small_all.at[dp], s_send.at[n], s_recv.at[n], peer)
        small_all[dp] = small[...]

    work = [norm_back] + [functools.partial(heads_back, n) for n in range(query_width // TILE)]
    work += [functools.partial(attend_back, head) for head in range(group_heads)]
    work += [keys_back] + [functools.partial(inputs_back, i) for i in range(2)]
    work += [functools.partial(weights_back, i) for i in range(shards // 4)] + [leave]

    mlp_count = len(units)
    need(1)
    line_terms(0)
    units += [(0, k) for k in ks]
    for i in range(-AHEAD, len(units) + LAG):
        if i + AHEAD == mlp_count:
            while work:
                work.pop(0)()
        if 0 <= i + AHEAD < len(units):
            first(*units[i + AHEAD])
        if 0 <= i < len(units):
            relay(*units[i])
        if 0 <= i - LAG:
            last(*units[i - LAG])
        if i in LINE_STEPS:
            line_terms(LINE_STEPS.index(i) + 1)
        for _ in range(PIECES):
            if work:
                work.pop(0)()
    for n, (kz, kp) in enumerate(masks):
        landed(small_all.at[flipped(z, kz) * PLANE + flipped(p, kp)], s_recv.at[n])
    total = small_all[0]
    for i in range(1, shards):
        total = total + small_all[i]
    staged[...] = total
    small_sum[c] = total
    send(staged, small_sum.at[c], s_send.at[len(masks)], s_recv.at[len(masks)], pair)
    line_total()
    landed(small_sum.at[1 - c], s_recv.at[len(masks)])
    total = attn_slots[0, 1].astype(F32)
    for k in others:
        landed(attn_line.at[k], z_recv.at[0, k])
        total = total + attn_line[k].astype(F32)
    attn_sum[...] = total
    for s in (1, 2, 3):
        for k in others:
            landed(outs[s].at[flipped(z, k)], z_recv.at[s, k])
    line_end()
    for copy in local:
        copy.wait()
    for copy in sent:
        copy.wait_send()


def reduce_all(quarters, mlp_grads, inputs):
    shards = quarters * PLANE
    dma = pltpu.SemaphoreType.DMA
    depth, part_cols = mlp_grads[0].shape[1:]
    y_half, _, r1, _, vec_sum, cosine, _, _, aset_all, q_in = inputs[:10]
    rows, width = r1.shape
    tokens, query_width = q_in.shape
    head_dim = cosine.shape[1]
    qkv_width = query_width + 2 * head_dim
    attn_shape = aset_all.shape[1:]
    vec_shape = vec_sum.shape
    vmem = pl.BlockSpec(memory_space=pltpu.VMEM)
    hbm = pl.BlockSpec(memory_space=pltpu.HBM)
    shape = jax.ShapeDtypeStruct
    quarter_out = shape((quarters, depth, part_cols), BF)
    return pl.pallas_call(
        functools.partial(reduce_kernel, quarters),
        out_shape=(
            shape((2,) + vec_shape, F32),
            shape(attn_shape, F32),
            shape((rows, width), F32),
            shape((rows, width), F32),
            quarter_out,
            quarter_out,
            quarter_out,
        ),
        in_specs=[hbm] * (3 + INPUTS),
        out_specs=[vmem] * 4 + [hbm] * 3,
        scratch_shapes=[
            pltpu.VMEM(vec_shape, F32),
            pltpu.VMEM((shards,) + vec_shape, F32),
            pltpu.VMEM(vec_shape, F32),
            pltpu.VMEM((quarters, 3) + attn_shape, BF),
            pltpu.VMEM((3, quarters, 3, depth, part_cols), BF),
            pltpu.VMEM((3, quarters, 2, depth, part_cols), BF),
            pltpu.VMEM((quarters,) + attn_shape, BF),
            pltpu.VMEM((2, quarters, rows, width), BF),
            pltpu.VMEM((shards,) + attn_shape, BF),
            pltpu.VMEM((2, rows, width), BF),
            pltpu.VMEM((rows, width), F32),
            pltpu.VMEM((tokens, query_width), BF),
            pltpu.VMEM((tokens, qkv_width), BF),
            pltpu.VMEM((tokens, head_dim), F32),
            pltpu.VMEM((tokens, head_dim), F32),
            pltpu.VMEM((2, rows, width), F32),
            pltpu.VMEM((rows, width), BF),
            pltpu.VMEM((rows, width), BF),
        ]
        + [pltpu.VMEM(x.shape, x.dtype) for x in inputs]
        + [
            dma((4, quarters, 3)),
            dma((4, quarters, 3)),
            dma((4, quarters)),
            dma((4, quarters)),
            dma((shards,)),
            dma((shards,)),
            dma((2, quarters)),
            dma((2, quarters)),
            dma((2,)),
            dma((2,)),
            dma((4,)),
            dma((3, quarters, 2)),
            dma((INPUTS,)),
        ],
        compiler_params=pltpu.CompilerParams(
            collective_id=1, has_side_effects=True, vmem_limit_bytes=62 * 2**20
        ),
    )(*mlp_grads, *inputs)


def local(
    hidden_in,
    row_lengths,
    norm_attn,
    w_query,
    b_query,
    w_key,
    b_key,
    w_value,
    b_value,
    w_out,
    norm_mlp,
    w_gate,
    w_up,
    w_down,
    out_grad,
):
    quarters = lax.axis_size("z")
    lanes = lax.axis_size("head")
    shards = quarters * PLANE
    copies = lax.axis_size("o")
    if copies > 1:
        norm_attn, norm_mlp, w_query, w_key, w_value, w_gate, w_up = [
            lax.all_gather(x, "o", axis=0, tiled=True)
            for x in (norm_attn, norm_mlp, w_query, w_key, w_value, w_gate, w_up)
        ]
        b_query, b_key, b_value, w_out, w_down = [
            lax.all_gather(x, "o", axis=1, tiled=True)
            for x in (b_query, b_key, b_value, w_out, w_down)
        ]
    token_count = hidden_in.shape[0] * lanes
    depth = norm_attn.shape[0]
    width = hidden_in.shape[1]
    head_dim = w_key.shape[1]
    query_width = w_query.shape[1]
    hidden_width = w_gate.shape[1]
    part_width = -(-hidden_width // (LANE * quarters)) * LANE
    segment, positions = layout(row_lengths[0], token_count)
    place = jnp.arange(token_count, dtype=jnp.int32)
    allowed = (segment[:, None] == segment[None, :]) & (place[None, :] <= place[:, None])
    tables = rotary_tables(positions, head_dim) + (jnp.where(allowed, 0.0, MASKED).astype(F32),)

    shard = lax.axis_index("z") * PLANE + lax.axis_index("p")

    def placed(part):
        mine = jnp.arange(shards, dtype=jnp.int32)[:, None] == shard
        return jnp.where(mine, part[None, :], 0).astype(BF).reshape(-1, LANE)

    vec = jnp.concatenate(
        [placed(x) for x in (norm_attn, norm_mlp, b_query[0], b_key[0], b_value[0])], 0
    )
    aset_all, vec_sum, wg, wu, wd, grad_rows, h1_all, *heads, residual, mlp_low = gather_all(
        jnp.concatenate([w_query, w_key, w_value, w_out.T], 1),
        vec,
        w_gate,
        w_up,
        w_down.T,
        out_grad,
        hidden_in,
        *tables,
        quarters,
        part_width,
    )
    y_half, dh2, *mlp_grads = mlp_all(
        mlp_low,
        grad_rows.reshape(quarters, token_count, width),
        *[w.reshape(width, part_width) for w in (wg, wu, wd)],
        hidden_width,
    )
    small_total, attn_part, block_out, grad_in, *quarter_grads = reduce_all(
        quarters,
        [g.reshape(shards, depth, part_width) for g in mlp_grads],
        (y_half, dh2, residual, out_grad, vec_sum, *tables, aset_all, *heads[:3], hidden_in, h1_all, heads[3]),
    )

    def whole_rows(parts):
        taken = []
        for index in range(quarters):
            skip = max(0, index * part_width - (hidden_width - part_width))
            if skip < part_width:
                taken.append(parts[index][:, skip:])
        return jnp.concatenate(taken, 1).astype(F32)

    grad_w_gate, grad_w_up, grad_w_down = [whole_rows(parts) for parts in quarter_grads]
    if copies > 1:
        small_total = lax.psum(small_total, "o")
        attn_part, grad_w_gate, grad_w_up, grad_w_down = [
            lax.psum_scatter(x, "o", scatter_dimension=0, tiled=True)
            for x in (attn_part, grad_w_gate, grad_w_up, grad_w_down)
        ]
    small_total = small_total.reshape(lanes, -1)
    gain_total = jnp.sum(small_total[:, : 2 * width], 0).reshape(2, width)
    bias_total = small_total[:, 2 * width :]
    return (
        block_out,
        grad_in,
        gain_total[0],
        attn_part[:, :query_width],
        bias_total[:, :query_width],
        attn_part[:, query_width : query_width + head_dim],
        bias_total[:, query_width : query_width + head_dim],
        attn_part[:, query_width + head_dim : query_width + 2 * head_dim],
        bias_total[:, query_width + head_dim :],
        attn_part[:, query_width + 2 * head_dim :].T,
        gain_total[1],
        grad_w_gate,
        grad_w_up,
        grad_w_down.T,
    )


def solution(mesh):
    shards = mesh.shape["dp"]
    copies = max(1, shards // (PLANE * PLANE))
    shape = (shards // (PLANE * copies), PLANE, copies, mesh.shape["head"])
    split = jax.sharding.Mesh(mesh.devices.reshape(shape), DP + ("head",))
    rows = P(DP + ("head",), None)
    deep = P(DP, "head")
    wide = P("head", DP)
    return jax.shard_map(
        local,
        mesh=split,
        in_specs=(
            rows,
            P(DP, None),
            P(DP),
            deep,
            wide,
            deep,
            wide,
            deep,
            wide,
            wide,
            P(DP),
            deep,
            deep,
            wide,
            rows,
        ),
        out_specs=(
            rows,
            rows,
            P(),
            deep,
            P(),
            deep,
            P(),
            deep,
            P(),
            wide,
            P(),
            deep,
            deep,
            wide,
        ),
        check_vma=False,
    )
```
